512 devices in a mesh: dp: 64 (over x_hi, z, core), mp: 8 (over x_lo, y).
Axes of the slice: x: 4 (x_hi: 2, x_lo: 2; x = x_hi * 2 + x_lo), y: 4, z: 16, core: 2. Of those that a mesh axis runs over, the one named last changes fastest.
Arguments:
- layer_input: bfloat16 [256, 256, 1536], P('dp', 'mp'), may hold values from -6 to 6
- in_weight: bfloat16 [1536, 4096], P('dp', 'mp'), may hold values from -0.15625 to 0.15625
- out_weight: bfloat16 [4096, 1536], P('mp'), may hold values from -0.09375 to 0.09375
- image_rest: bfloat16 [1792, 1536], P('dp'), may hold values from -2 to 2
- text_embed: bfloat16 [2048, 1536], P(('dp', 'mp')), may hold values from -2 to 2
- log_scale: float32 [1], replicated, may hold values from 3.4 to 4.6
- logit_bias: float32 [1], replicated, may hold values from -6 to -2
- loss_scale: float32 [1], replicated, may hold values from 2048 to 8192
Outputs:
- input_grad: bfloat16 [256, 256, 1536], P('dp', 'mp')
- in_weight_grad: bfloat16 [1536, 4096], P(None, 'mp')
- out_weight_grad: bfloat16 [4096, 1536], P('mp', 'dp')
- rest_grad: float32 [1792, 1536], P('dp')
- text_grad: float32 [2048, 1536], P(('dp', 'mp'))
The draws below stay inside these ranges and needn't reach their ends.
All inputs are finite; a program needn't handle non-finite values.
Results may differ from the reference program's by a relative error of at most 0.025.
Values may be sent and summed in bfloat16 or wider, within the bound.
No kernel may reach another device: no remote copies, remote signals or barrier semaphores. Data moves between devices by JAX's collectives and lax.ppermute only.
A program may use at most 64 MiB of HBM per device.

```python
import math
import jax
import jax.numpy as jnp
from jax import lax

D = 1536
FF = 4096
PATCHES = 256
MICRO = 4
IMG_DP = 32
REST = 28
BATCH = 2048
LAYER_ROWS = 256
N_DP = 64
N_MP = 8


def steps_of(stream_key, shape, shards, smallest, high):
    loudness = 1.0
    for dim, blocks in shards:
        draws = jax.random.uniform(jax.random.fold_in(jax.random.fold_in(stream_key, 6), dim), (blocks,), jnp.float32, smallest / len(shards), high / len(shards))
        loudness = loudness * jnp.repeat(jnp.exp(draws), shape[dim] // blocks).reshape((-1,) + (1,) * (len(shape) - 1 - dim))
    return loudness


def gaussian(stream_key, extent, scale, most, cuts=(), kind=jnp.bfloat16):
    gain = steps_of(stream_key, extent, cuts, -0.22, 0.18) if cuts else 1.0
    entries = jax.random.normal(stream_key, extent, jnp.float32) * scale * gain
    return jnp.minimum(jnp.maximum(entries, -most), most).astype(kind)


def setup_inputs(seed: int = 0) -> dict:
    key_list = jax.random.split(jax.random.key(seed), 9)
    return {
        "layer_input": gaussian(key_list[0], (LAYER_ROWS, PATCHES, D), 1.0, 6.0, ((0, 64), (1, 8))),
        "in_weight": gaussian(key_list[1], (D, FF), D ** -0.5, 0.15625, ((0, 64), (1, 8))),
        "out_weight": gaussian(key_list[2], (FF, D), FF ** -0.5, 0.09375, ((0, 8),)),
        "image_rest": gaussian(key_list[3], (N_DP * REST, D), 0.3, 2.0, ((0, 64),)),
        "text_embed": gaussian(key_list[4], (BATCH, D), 0.3, 2.0, ((0, 512),)),
        "log_scale": jnp.clip(jax.random.uniform(key_list[5], (1,), jnp.float32, 3.4, 4.6), 3.4, 4.6),
        "logit_bias": jnp.clip(jax.random.uniform(key_list[6], (1,), jnp.float32, -6.0, -2.0), -6.0, -2.0),
        "loss_scale": jnp.clip(jnp.exp(jax.random.uniform(key_list[7], (1,), jnp.float32, math.log(2048.0), math.log(8192.0))), 2048.0, 8192.0),
    }


epsilon = 1e-06

def gelu_slope(values):
    root = math.sqrt(2.0 / math.pi)
    inner = root * (values + 0.044715 * values * values * values)
    tangent = jnp.tanh(inner)
    return 0.5 * (1.0 + tangent) + 0.5 * values * (1.0 - tangent * tangent) * root * (1.0 + 3.0 * 0.044715 * values * values)

def unit_rows(values):
    norm_inv = lax.rsqrt(lax.optimization_barrier(jnp.sum(values * values, -1, keepdims=True)) + epsilon)
    return (values * norm_inv, norm_inv)

def unit_backward(grad_dir, unit_vals, norm_inv):
    return (grad_dir - unit_vals * lax.optimization_barrier(jnp.sum(unit_vals * grad_dir, -1, keepdims=True))) * norm_inv

def reference(layer_input, in_weight, out_weight, image_rest, text_embed, log_scale, logit_bias, loss_scale):
    inputs_f = layer_input.astype(jnp.float32)
    centered = inputs_f - lax.optimization_barrier(jnp.mean(inputs_f, -1, keepdims=True))
    inv_std = lax.rsqrt(lax.optimization_barrier(jnp.mean(centered * centered, -1, keepdims=True)) + epsilon)
    standard = centered * inv_std
    normed = standard.astype(jnp.bfloat16)
    flat = normed.reshape(-1, D)
    hidden = jnp.dot(flat, in_weight, preferred_element_type=jnp.float32)
    act_mean = lax.optimization_barrier(jnp.mean(jax.nn.gelu(hidden, approximate=True).reshape(LAYER_ROWS, PATCHES, FF), 1)).astype(jnp.bfloat16)
    pooled = lax.optimization_barrier(jnp.mean(inputs_f, 1)) + jnp.dot(act_mean, out_weight, preferred_element_type=jnp.float32)
    images = jnp.concatenate([pooled.reshape(N_DP, MICRO, D), image_rest.astype(jnp.float32).reshape(N_DP, REST, D)], 1).reshape(BATCH, D)
    image_unit, image_inv = unit_rows(images)
    image_low = image_unit.astype(jnp.bfloat16)
    text_unit, text_inv = unit_rows(text_embed.astype(jnp.float32))
    text_low = text_unit.astype(jnp.bfloat16)
    scale_value = jnp.exp(log_scale[0])
    weight_coef = loss_scale[0] / BATCH
    logits = scale_value * jnp.dot(image_low, text_low.T, preferred_element_type=jnp.float32) + logit_bias[0]
    pair_weights = (weight_coef * jax.nn.sigmoid(logits)).astype(jnp.bfloat16)
    image_dir = scale_value * (jnp.dot(pair_weights, text_low, preferred_element_type=jnp.float32) - weight_coef * text_low.astype(jnp.float32))
    text_dir = scale_value * (jnp.dot(pair_weights.T, image_low, preferred_element_type=jnp.float32) - weight_coef * image_low.astype(jnp.float32))
    image_grad = unit_backward(image_dir, image_unit, image_inv).reshape(N_DP, IMG_DP, D)
    text_grad = unit_backward(text_dir, text_unit, text_inv)
    pool_grad = image_grad[:, :MICRO].reshape(LAYER_ROWS, D)
    rest_grad = image_grad[:, MICRO:].reshape(N_DP * REST, D)
    pool_low = pool_grad.astype(jnp.bfloat16)
    row_grad = jnp.dot(pool_low, out_weight.T, preferred_element_type=jnp.float32) / PATCHES
    hidden_grad = (row_grad.reshape(LAYER_ROWS, 1, FF) * gelu_slope(hidden).reshape(LAYER_ROWS, PATCHES, FF)).astype(jnp.bfloat16).reshape(-1, FF)
    in_weight_grad = jnp.dot(flat.T, hidden_grad, preferred_element_type=jnp.float32).astype(jnp.bfloat16)
    out_weight_grad = jnp.dot(act_mean.T, pool_low, preferred_element_type=jnp.float32).astype(jnp.bfloat16)
    block_width = FF // N_MP

    def shard_term(total, shard):
        start_unit = (shard * block_width).astype(jnp.int32)
        columns = lax.dynamic_slice_in_dim(hidden_grad, start_unit, block_width, 1)
        weight_cols = lax.dynamic_slice_in_dim(in_weight, start_unit, block_width, 1)
        term = jnp.dot(columns, weight_cols.T, preferred_element_type=jnp.float32).astype(jnp.bfloat16)
        return (total + term.astype(jnp.float32), None)
    normed_grad, _ = lax.scan(shard_term, jnp.zeros((LAYER_ROWS * PATCHES, D), jnp.float32), jnp.arange(N_MP, dtype=jnp.int32))
    normed_grad = normed_grad.reshape(LAYER_ROWS, PATCHES, D)
    input_grad = inv_std * (normed_grad - lax.optimization_barrier(jnp.mean(normed_grad, -1, keepdims=True)) - standard * lax.optimization_barrier(jnp.mean(normed_grad * standard, -1, keepdims=True)))
    input_grad = (input_grad + pool_grad[:, None, :] / PATCHES).astype(jnp.bfloat16)
    return (input_grad, in_weight_grad, out_weight_grad, rest_grad, text_grad)
```

```python
import math

import jax
import jax.numpy as jnp
from jax import lax
from jax.sharding import PartitionSpec as P

epsilon = 1e-06
GROUPS = {
    "core": [[2 * k, 2 * k + 1] for k in range(32)],
    "x_hi": [[k, 32 + k] for k in range(32)],
    "z": [[32 * high + 2 * z + core for z in range(16)] for high in range(2) for core in range(2)],
}


def gelu_slope(values):
    root = math.sqrt(2.0 / math.pi)
    inner = root * (values + 0.044715 * values * values * values)
    tangent = jnp.tanh(inner)
    return 0.5 * (1.0 + tangent) + 0.5 * values * (1.0 - tangent * tangent) * root * (
        1.0 + 3.0 * 0.044715 * values * values
    )


def unit_rows(values):
    norm_inv = lax.rsqrt(jnp.sum(values * values, -1, keepdims=True) + epsilon)
    return (values * norm_inv, norm_inv)


def unit_backward(grad_dir, unit_vals, norm_inv):
    return (grad_dir - unit_vals * jnp.sum(unit_vals * grad_dir, -1, keepdims=True)) * norm_inv


def exchange(blocks, axis):
    if axis in GROUPS:
        return lax.all_to_all(blocks, "dp", 0, 0, axis_index_groups=GROUPS[axis], tiled=True)
    return lax.all_to_all(blocks, axis, 0, 0, tiled=True)


def spread(block, axis):
    count = len(GROUPS[axis][0]) if axis in GROUPS else lax.axis_size(axis)
    return exchange(jnp.broadcast_to(block[None], (count,) + block.shape), axis)


def sum_over(block, axis):
    return jnp.sum(spread(block, axis).astype(jnp.float32), 0)


def gather_dp(block):
    rows, width = block.shape
    block = lax.all_gather(block, "dp", axis=0, axis_index_groups=GROUPS["z"], tiled=True)
    block = spread(block, "x_hi")
    block = spread(block.reshape(-1, width), "core")
    return block.reshape(2, 2, 16, rows, width)


def scatter_sum_dp(parts):
    rows, width = parts.shape[-2:]
    for axis in ("core", "x_hi"):
        got = exchange(parts, axis)
        parts = jnp.sum(got.astype(jnp.float32), 0).astype(jnp.bfloat16)
    return jnp.sum(exchange(parts, "z").astype(jnp.float32), 0).reshape(rows, width)


def body(
    layer_input, in_weight, out_weight, image_rest, text_embed, log_scale, logit_bias, loss_scale
):
    local_rows, local_patches, width_model = layer_input.shape
    hidden_width = in_weight.shape[1]
    patches = local_patches * 8
    dp_count = 64
    in_rows = in_weight.shape[0]
    text_count = text_embed.shape[0]
    text_rows = text_count * width_model // hidden_width

    inputs_f = layer_input.astype(jnp.float32)
    centered = inputs_f - jnp.mean(inputs_f, -1, keepdims=True)
    inv_std = lax.rsqrt(jnp.mean(centered * centered, -1, keepdims=True) + epsilon)
    standard = centered * inv_std
    flat = lax.all_gather(
        standard.astype(jnp.bfloat16).reshape(-1, width_model), "mp", axis=0, tiled=True
    )
    token_shape = (8, local_rows, local_patches, hidden_width)

    text_unit, text_inv = unit_rows(text_embed.astype(jnp.float32))
    text_low = text_unit.astype(jnp.bfloat16)
    both = gather_dp(jnp.concatenate([in_weight, text_low.reshape(text_rows, hidden_width)], 0))
    full_in = jnp.transpose(both[:, :, :, :in_rows], (1, 2, 0, 3, 4)).reshape(
        width_model, hidden_width
    )
    texts = both[:, :, :, in_rows:].reshape(dp_count * text_count, width_model)

    hidden = jnp.dot(flat, full_in, preferred_element_type=jnp.float32)
    act_mean = jnp.mean(
        jax.nn.gelu(hidden, approximate=True).reshape(token_shape), (0, 2)
    ).astype(jnp.bfloat16)
    part_pool = (
        jnp.dot(act_mean, out_weight, preferred_element_type=jnp.float32)
        + jnp.sum(inputs_f, 1) / patches
    )
    pooled = sum_over(part_pool, "mp")
    images = jnp.concatenate([pooled, image_rest.astype(jnp.float32)], 0)
    image_count = images.shape[0]
    image_unit, image_inv = unit_rows(images)
    image_low = image_unit.astype(jnp.bfloat16)
    scale_value = jnp.exp(log_scale[0])
    weight_coef = loss_scale[0] / (image_count * dp_count)

    logits = (
        scale_value * jnp.einsum("id,jd->ij", image_low, texts, preferred_element_type=jnp.float32)
        + logit_bias[0]
    )
    pair_weights = (weight_coef * jax.nn.sigmoid(logits)).astype(jnp.bfloat16)
    image_acc = jnp.dot(pair_weights, texts, preferred_element_type=jnp.float32)
    text_part = jnp.einsum("ij,id->jd", pair_weights, image_low, preferred_element_type=jnp.float32)

    first_row = lax.axis_index("mp") * text_count
    zero_index = jnp.zeros((), jnp.int32)
    paired_texts = lax.dynamic_update_slice(
        jnp.zeros_like(images), text_low.astype(jnp.float32), (first_row, zero_index)
    )
    image_dir = scale_value * sum_over(
        (image_acc - weight_coef * paired_texts).astype(jnp.bfloat16), "mp"
    )
    image_grad = unit_backward(image_dir, image_unit, image_inv)
    pool_grad = image_grad[:local_rows]
    rest_grad = image_grad[local_rows:]
    pool_low = pool_grad.astype(jnp.bfloat16)
    row_grad = (
        jnp.einsum("bd,fd->bf", pool_low, out_weight, preferred_element_type=jnp.float32) / patches
    )
    hidden_grad = (
        row_grad.reshape(1, local_rows, 1, hidden_width) * gelu_slope(hidden).reshape(token_shape)
    ).astype(jnp.bfloat16).reshape(-1, hidden_width)
    normed_part = jnp.einsum(
        "rf,df->rd", hidden_grad, full_in, preferred_element_type=jnp.float32
    ).astype(jnp.bfloat16)
    normed_grad = (
        lax.psum_scatter(normed_part, "mp", scatter_dimension=0, tiled=True)
        .astype(jnp.float32)
        .reshape(layer_input.shape)
    )

    in_part = jnp.einsum(
        "rd,rf->df", flat, hidden_grad, preferred_element_type=jnp.float32
    ).astype(jnp.bfloat16)
    summed = scatter_sum_dp(
        jnp.concatenate(
            [
                in_part.reshape(2, 2, 16, in_rows, hidden_width),
                text_part.astype(jnp.bfloat16).reshape(2, 2, 16, text_rows, hidden_width),
            ],
            3,
        )
    )
    text_acc = summed[in_rows:].reshape(text_count, width_model)
    paired_images = lax.dynamic_slice_in_dim(image_low, first_row, text_count, 0).astype(
        jnp.float32
    )
    text_dir = scale_value * (text_acc - weight_coef * paired_images)
    text_grad = unit_backward(text_dir, text_unit, text_inv)

    column_width = width_model // dp_count
    columns = exchange(
        jnp.transpose(pool_low.reshape(local_rows, dp_count, column_width), (1, 0, 2)), "dp"
    )
    columns = jnp.transpose(
        columns.reshape(2, 16, 2, local_rows, column_width), (2, 0, 1, 3, 4)
    ).reshape(dp_count * local_rows, column_width)

    back = gather_dp(jnp.concatenate([summed[:in_rows].astype(jnp.bfloat16), act_mean], 0))
    in_weight_grad = back[:, :, :, :in_rows].reshape(width_model, hidden_width)
    all_means = back[:, :, :, in_rows:].reshape(dp_count * local_rows, hidden_width)
    out_weight_grad = jnp.einsum(
        "bf,bc->fc", all_means, columns, preferred_element_type=jnp.float32
    ).astype(jnp.bfloat16)

    input_grad = inv_std * (
        normed_grad
        - jnp.mean(normed_grad, -1, keepdims=True)
        - standard * jnp.mean(normed_grad * standard, -1, keepdims=True)
    )
    input_grad = (input_grad + pool_grad[:, None, :] / patches).astype(jnp.bfloat16)
    return (input_grad, in_weight_grad, out_weight_grad, rest_grad, text_grad)


def solution(mesh):
    in_specs = (
        P("dp", "mp", None),
        P("dp", "mp"),
        P("mp", None),
        P("dp", None),
        P(("dp", "mp"), None),
        P(),
        P(),
        P(),
    )
    out_specs = (
        P("dp", "mp", None),
        P(None, "mp"),
        P("mp", "dp"),
        P("dp", None),
        P(("dp", "mp"), None),
    )
    return jax.shard_map(body, mesh=mesh, in_specs=in_specs, out_specs=out_specs, check_vma=False)
```

```python
import math

import jax
import jax.numpy as jnp
from jax import lax
from jax.sharding import PartitionSpec as P

epsilon = 1e-06


def dp_index(x_hi, z_hi, z_lo, core):
    return 32 * x_hi + 4 * z_hi + 2 * z_lo + core


TWO, EIGHT = range(2), range(8)
GROUPS = {
    "core": [[dp_index(x, h, l, c) for c in TWO] for x in TWO for h in EIGHT for l in TWO],
    "x_hi": [[dp_index(x, h, l, c) for x in TWO] for h in EIGHT for l in TWO for c in TWO],
    "z": [[dp_index(x, h, l, c) for h in EIGHT for l in TWO] for x in TWO for c in TWO],
    "z_hi": [[dp_index(x, h, l, c) for h in EIGHT] for x in TWO for l in TWO for c in TWO],
    "x_hi z_lo": [[dp_index(x, h, l, c) for x in TWO for l in TWO] for h in EIGHT for c in TWO],
    "core x_hi": [[dp_index(x, h, l, c) for c in TWO for x in TWO] for h in EIGHT for l in TWO],
}


def gelu_slope(values):
    root = math.sqrt(2.0 / math.pi)
    inner = root * (values + 0.044715 * values * values * values)
    tangent = jnp.tanh(inner)
    return 0.5 * (1.0 + tangent) + 0.5 * values * (1.0 - tangent * tangent) * root * (
        1.0 + 3.0 * 0.044715 * values * values
    )


def unit_rows(values):
    norm_inv = lax.rsqrt(jnp.sum(values * values, -1, keepdims=True) + epsilon)
    return (values * norm_inv, norm_inv)


def unit_backward(grad_dir, unit_vals, norm_inv):
    return (grad_dir - unit_vals * jnp.sum(unit_vals * grad_dir, -1, keepdims=True)) * norm_inv


def exchange(blocks, axis):
    if axis in GROUPS:
        return lax.all_to_all(blocks, "dp", 0, 0, axis_index_groups=GROUPS[axis], tiled=True)
    return lax.all_to_all(blocks, axis, 0, 0, tiled=True)


def spread(block, axis):
    count = len(GROUPS[axis][0]) if axis in GROUPS else lax.axis_size(axis)
    return exchange(jnp.broadcast_to(block[None], (count,) + block.shape), axis)


def sum_over(block, axis):
    return jnp.sum(spread(block, axis).astype(jnp.float32), 0)


def gather_z(block):
    return lax.all_gather(block, "dp", axis=0, axis_index_groups=GROUPS["z"], tiled=False)


def pad_rows(block, rows):
    return jnp.pad(block, [(0, 0)] * (block.ndim - 2) + [(0, rows - block.shape[-2]), (0, 0)])


def body(
    layer_input, in_weight, out_weight, image_rest, text_embed, log_scale, logit_bias, loss_scale
):
    local_rows, local_patches, width_model = layer_input.shape
    hidden_width = in_weight.shape[1]
    patches = local_patches * 8
    dp_count = 64
    in_rows = in_weight.shape[0]
    text_count = text_embed.shape[0]
    text_rows = text_count * width_model // hidden_width
    scale_value = jnp.exp(log_scale[0])
    image_count = local_rows + image_rest.shape[0]
    weight_coef = loss_scale[0] / (image_count * dp_count)

    inputs_f = layer_input.astype(jnp.float32)
    centered = inputs_f - jnp.mean(inputs_f, -1, keepdims=True)
    inv_std = lax.rsqrt(jnp.mean(centered * centered, -1, keepdims=True) + epsilon)
    standard = centered * inv_std
    normed = standard.astype(jnp.bfloat16).reshape(-1, width_model)
    in_weight, normed = lax.optimization_barrier((in_weight, normed))
    flat = lax.all_gather(normed, "mp", axis=0, tiled=True)
    token_shape = (8, local_rows, local_patches, hidden_width)

    text_unit, text_inv = unit_rows(text_embed.astype(jnp.float32))
    text_low = text_unit.astype(jnp.bfloat16)
    pair = spread(in_weight, "x_hi").reshape(2 * in_rows, hidden_width)
    both = gather_z(jnp.concatenate([pair, text_low.reshape(text_rows, hidden_width)], 0))
    full_in = spread(both[:, : 2 * in_rows], "core").reshape(2, 16, 2, in_rows, hidden_width)
    full_in = jnp.transpose(full_in, (2, 1, 0, 3, 4)).reshape(width_model, hidden_width)
    flat, late = lax.optimization_barrier((flat, both[:, 2 * in_rows :]))
    texts = spread(late, "core x_hi")

    first_row = lax.axis_index("mp") * text_count
    zero_index = jnp.zeros((), jnp.int32)
    paired_texts = lax.dynamic_update_slice(
        jnp.zeros((image_count, width_model), jnp.float32),
        text_low.astype(jnp.float32),
        (first_row, zero_index),
    )
    hidden = jnp.dot(flat, full_in, preferred_element_type=jnp.float32)
    act_mean = jnp.mean(
        jax.nn.gelu(hidden, approximate=True).reshape(token_shape), (0, 2)
    ).astype(jnp.bfloat16)
    act_mean, texts = lax.optimization_barrier((act_mean, texts))
    texts = jnp.transpose(texts.reshape(4, 8, 2, text_rows, hidden_width), (0, 2, 1, 3, 4))
    texts = texts.reshape(dp_count * text_count, width_model)
    part_pool = (
        jnp.dot(act_mean, out_weight, preferred_element_type=jnp.float32)
        + jnp.sum(inputs_f, 1) / patches
    )
    pooled = sum_over(part_pool, "mp")
    images = jnp.concatenate([pooled, image_rest.astype(jnp.float32)], 0)
    image_unit, image_inv = unit_rows(images)
    image_low = image_unit.astype(jnp.bfloat16)
    logits = (
        scale_value * jnp.einsum("id,jd->ij", image_low, texts, preferred_element_type=jnp.float32)
        + logit_bias[0]
    )
    pair_weights = (weight_coef * jax.nn.sigmoid(logits)).astype(jnp.bfloat16)
    image_acc = jnp.dot(pair_weights, texts, preferred_element_type=jnp.float32)
    image_dir = scale_value * sum_over(
        (image_acc - weight_coef * paired_texts).astype(jnp.bfloat16), "mp"
    )
    image_grad = unit_backward(image_dir, image_unit, image_inv)
    pool_grad = image_grad[:local_rows]
    rest_grad = image_grad[local_rows:]
    pool_low = pool_grad.astype(jnp.bfloat16)
    row_grad = (
        jnp.einsum("bd,fd->bf", pool_low, out_weight, preferred_element_type=jnp.float32) / patches
    )
    hidden_grad = (
        (row_grad.reshape(1, local_rows, 1, hidden_width) * gelu_slope(hidden).reshape(token_shape))
        .astype(jnp.bfloat16)
        .reshape(-1, hidden_width)
    )

    text_part = jnp.einsum("ij,id->jd", pair_weights, image_low, preferred_element_type=jnp.float32)
    in_part = jnp.einsum("rd,rf->df", flat, hidden_grad, preferred_element_type=jnp.float32)
    index = lax.axis_index("dp")
    place = index % 2 * 4 + index // 32 * 2 + index // 2 % 2
    column_width = width_model // dp_count
    columns = pool_low.reshape(local_rows, 2, 8, 2, 2, column_width)
    columns = jnp.transpose(columns, (4, 1, 3, 2, 0, 5)).reshape(2, 4, 8, local_rows, column_width)
    columns = jnp.concatenate([columns] * 8, -1)
    columns = jnp.where(jnp.arange(8 * column_width) // column_width == place, columns, 0)
    columns = jnp.pad(columns, [(0, 0)] * 4 + [(0, hidden_width - columns.shape[-1])])
    parts = jnp.concatenate(
        [
            in_part.astype(jnp.bfloat16).reshape(2, 4, 8, in_rows, hidden_width),
            text_part.astype(jnp.bfloat16).reshape(2, 4, 8, text_rows, hidden_width),
            columns,
        ],
        3,
    )
    for axis in ("core", "x_hi z_lo"):
        got = exchange(parts, axis).astype(jnp.float32)
        parts = sum(got[k] for k in range(got.shape[0])).astype(jnp.bfloat16)
    hidden_grad, parts = lax.optimization_barrier((hidden_grad, parts))
    normed_part = jnp.einsum(
        "rf,df->rd", hidden_grad, full_in, preferred_element_type=jnp.float32
    ).astype(jnp.bfloat16)
    normed_grad = (
        lax.psum_scatter(normed_part, "mp", scatter_dimension=0, tiled=True)
        .astype(jnp.float32)
        .reshape(layer_input.shape)
    )
    got = exchange(parts, "z_hi")
    summed = jnp.sum(got[:, : in_rows + text_rows].astype(jnp.float32), 0)
    back = jnp.concatenate([summed[:in_rows].astype(jnp.bfloat16), act_mean], 0)
    back = spread(spread(spread(pad_rows(back, 32), "z_hi"), "x_hi z_lo"), "core")
    back = back.reshape(dp_count, 32, hidden_width)
    in_weight_grad = back[:, :in_rows].reshape(width_model, hidden_width)
    all_means = back[:, in_rows : in_rows + local_rows].reshape(-1, hidden_width)
    columns = got[:, in_rows + text_rows :, : 8 * column_width]
    columns = columns.reshape(8, local_rows, 8, column_width)
    columns = jnp.transpose(columns, (2, 0, 1, 3)).reshape(-1, column_width)
    out_weight_grad = jnp.einsum(
        "bf,bc->fc", all_means, columns, preferred_element_type=jnp.float32
    ).astype(jnp.bfloat16)

    text_acc = summed[in_rows:].reshape(text_count, width_model)
    paired_images = lax.dynamic_slice_in_dim(image_low, first_row, text_count, 0).astype(
        jnp.float32
    )
    text_dir = scale_value * (text_acc - weight_coef * paired_images)
    text_grad = unit_backward(text_dir, text_unit, text_inv)

    input_grad = inv_std * (
        normed_grad
        - jnp.mean(normed_grad, -1, keepdims=True)
        - standard * jnp.mean(normed_grad * standard, -1, keepdims=True)
    )
    input_grad = (input_grad + pool_grad[:, None, :] / patches).astype(jnp.bfloat16)
    return (input_grad, in_weight_grad, out_weight_grad, rest_grad, text_grad)


def solution(mesh):
    in_specs = (
        P("dp", "mp", None),
        P("dp", "mp"),
        P("mp", None),
        P("dp", None),
        P(("dp", "mp"), None),
        P(),
        P(),
        P(),
    )
    out_specs = (
        P("dp", "mp", None),
        P(None, "mp"),
        P("mp", "dp"),
        P("dp", None),
        P(("dp", "mp"), None),
    )
    return jax.shard_map(body, mesh=mesh, in_specs=in_specs, out_specs=out_specs, check_vma=False)
```

```python
import math

import jax
import jax.numpy as jnp
from jax import lax
from jax.sharding import PartitionSpec as P

epsilon = 1e-06


def dp_index(x_hi, z_hi, z_lo, core):
    return 32 * x_hi + 4 * z_hi + 2 * z_lo + core


TWO, EIGHT = range(2), range(8)
GROUPS = {
    "core": [[dp_index(x, h, l, c) for c in TWO] for x in TWO for h in EIGHT for l in TWO],
    "x_hi": [[dp_index(x, h, l, c) for x in TWO] for h in EIGHT for l in TWO for c in TWO],
    "z": [[dp_index(x, h, l, c) for h in EIGHT for l in TWO] for x in TWO for c in TWO],
    "z_hi": [[dp_index(x, h, l, c) for h in EIGHT] for x in TWO for l in TWO for c in TWO],
    "x_hi z_lo": [[dp_index(x, h, l, c) for x in TWO for l in TWO] for h in EIGHT for c in TWO],
    "core x_hi": [[dp_index(x, h, l, c) for c in TWO for x in TWO] for h in EIGHT for l in TWO],
}


def gelu_slope(values):
    root = math.sqrt(2.0 / math.pi)
    inner = root * (values + 0.044715 * values * values * values)
    tangent = jnp.tanh(inner)
    return 0.5 * (1.0 + tangent) + 0.5 * values * (1.0 - tangent * tangent) * root * (
        1.0 + 3.0 * 0.044715 * values * values
    )


def unit_rows(values):
    norm_inv = lax.rsqrt(jnp.sum(values * values, -1, keepdims=True) + epsilon)
    return (values * norm_inv, norm_inv)


def unit_backward(grad_dir, unit_vals, norm_inv):
    return (grad_dir - unit_vals * jnp.sum(unit_vals * grad_dir, -1, keepdims=True)) * norm_inv


def exchange(blocks, axis):
    if axis in GROUPS:
        return lax.all_to_all(blocks, "dp", 0, 0, axis_index_groups=GROUPS[axis], tiled=True)
    return lax.all_to_all(blocks, axis, 0, 0, tiled=True)


def spread(block, axis):
    count = len(GROUPS[axis][0]) if axis in GROUPS else lax.axis_size(axis)
    return exchange(jnp.broadcast_to(block[None], (count,) + block.shape), axis)


def pair(block, axis):
    index = lax.axis_index("dp")
    first = (index % 2 if axis == "core" else index // 32) == 0
    other = lax.ppermute(block, "dp", [p for a, b in GROUPS[axis] for p in ((a, b), (b, a))])
    return jnp.stack([jnp.where(first, block, other), jnp.where(first, other, block)])


def sum_over(block, axis):
    return jnp.sum(spread(block, axis).astype(jnp.float32), 0)


def gather_z(block):
    return lax.all_gather(block, "dp", axis=0, axis_index_groups=GROUPS["z"], tiled=False)


def pad_rows(block, rows):
    return jnp.pad(block, [(0, 0)] * (block.ndim - 2) + [(0, rows - block.shape[-2]), (0, 0)])


def body(
    layer_input, in_weight, out_weight, image_rest, text_embed, log_scale, logit_bias, loss_scale
):
    local_rows, local_patches, width_model = layer_input.shape
    hidden_width = in_weight.shape[1]
    patches = local_patches * 8
    dp_count = 64
    in_rows = in_weight.shape[0]
    text_count = text_embed.shape[0]
    text_rows = text_count * width_model // hidden_width
    scale_value = jnp.exp(log_scale[0])
    image_count = local_rows + image_rest.shape[0]
    weight_coef = loss_scale[0] / (image_count * dp_count)

    inputs_f = layer_input.astype(jnp.float32)
    centered = inputs_f - jnp.mean(inputs_f, -1, keepdims=True)
    inv_std = lax.rsqrt(jnp.mean(centered * centered, -1, keepdims=True) + epsilon)
    standard = centered * inv_std
    normed = standard.astype(jnp.bfloat16).reshape(-1, width_model)
    token_shape = (8, local_rows, local_patches, hidden_width)

    text_unit, text_inv = unit_rows(text_embed.astype(jnp.float32))
    text_low = text_unit.astype(jnp.bfloat16)
    in_weight, normed = lax.optimization_barrier((in_weight, normed))
    near = pair(in_weight, "x_hi").reshape(2 * in_rows, hidden_width)
    near = jnp.concatenate([near, text_low.reshape(text_rows, hidden_width)], 0)
    flat = lax.all_gather(normed, "mp", axis=0, tiled=True)
    both = gather_z(near)
    full_in = pair(both[:, : 2 * in_rows], "core").reshape(2, 16, 2, in_rows, hidden_width)
    full_in = jnp.transpose(full_in, (2, 1, 0, 3, 4)).reshape(width_model, hidden_width)
    texts = spread(both[:, 2 * in_rows :], "core x_hi")

    first_row = lax.axis_index("mp") * text_count
    zero_index = jnp.zeros((), jnp.int32)
    paired_texts = lax.dynamic_update_slice(
        jnp.zeros((image_count, width_model), jnp.float32),
        text_low.astype(jnp.float32),
        (first_row, zero_index),
    )
    hidden = jnp.dot(flat, full_in, preferred_element_type=jnp.float32)
    act_mean = jnp.mean(
        jax.nn.gelu(hidden, approximate=True).reshape(token_shape), (0, 2)
    ).astype(jnp.bfloat16)
    act_mean, texts = lax.optimization_barrier((act_mean, texts))
    texts = jnp.transpose(texts.reshape(4, 8, 2, text_rows, hidden_width), (0, 2, 1, 3, 4))
    texts = texts.reshape(dp_count * text_count, width_model)
    part_pool = (
        jnp.dot(act_mean, out_weight, preferred_element_type=jnp.float32)
        + jnp.sum(inputs_f, 1) / patches
    )
    pooled = sum_over(part_pool, "mp")
    images = jnp.concatenate([pooled, image_rest.astype(jnp.float32)], 0)
    image_unit, image_inv = unit_rows(images)
    image_low = image_unit.astype(jnp.bfloat16)
    logits = (
        scale_value * jnp.einsum("id,jd->ij", image_low, texts, preferred_element_type=jnp.float32)
        + logit_bias[0]
    )
    pair_weights = (weight_coef * jax.nn.sigmoid(logits)).astype(jnp.bfloat16)
    image_acc = jnp.dot(pair_weights, texts, preferred_element_type=jnp.float32)
    image_dir = scale_value * sum_over(
        (image_acc - weight_coef * paired_texts).astype(jnp.bfloat16), "mp"
    )
    image_grad = unit_backward(image_dir, image_unit, image_inv)
    pool_grad = image_grad[:local_rows]
    rest_grad = image_grad[local_rows:]
    pool_low = pool_grad.astype(jnp.bfloat16)
    row_grad = (
        jnp.einsum("bd,fd->bf", pool_low, out_weight, preferred_element_type=jnp.float32) / patches
    )
    hidden_grad = (
        (row_grad.reshape(1, local_rows, 1, hidden_width) * gelu_slope(hidden).reshape(token_shape))
        .astype(jnp.bfloat16)
        .reshape(-1, hidden_width)
    )

    text_part = jnp.einsum("ij,id->jd", pair_weights, image_low, preferred_element_type=jnp.float32)
    in_part = jnp.einsum("rd,rf->df", flat, hidden_grad, preferred_element_type=jnp.float32)
    index = lax.axis_index("dp")
    place = index % 2 * 4 + index // 32 * 2 + index // 2 % 2
    column_width = width_model // dp_count
    columns = pool_low.reshape(local_rows, 2, 8, 2, 2, column_width)
    columns = jnp.transpose(columns, (4, 1, 3, 2, 0, 5)).reshape(2, 4, 8, local_rows, column_width)
    columns = jnp.concatenate([columns] * 8, -1)
    columns = jnp.where(jnp.arange(8 * column_width) // column_width == place, columns, 0)
    columns = jnp.pad(columns, [(0, 0)] * 4 + [(0, hidden_width - columns.shape[-1])])
    parts = jnp.concatenate(
        [
            in_part.astype(jnp.bfloat16).reshape(2, 4, 8, in_rows, hidden_width),
            text_part.astype(jnp.bfloat16).reshape(2, 4, 8, text_rows, hidden_width),
            columns,
        ],
        3,
    )
    for axis in ("core", "x_hi z_lo"):
        got = exchange(parts, axis).astype(jnp.float32)
        parts = sum(got[k] for k in range(got.shape[0])).astype(jnp.bfloat16)
    normed_part = jnp.einsum(
        "rf,df->rd", hidden_grad, full_in, preferred_element_type=jnp.float32
    ).astype(jnp.bfloat16)
    normed_part, parts = lax.optimization_barrier((normed_part, parts))
    normed_grad = (
        lax.psum_scatter(normed_part, "mp", scatter_dimension=0, tiled=True)
        .astype(jnp.float32)
        .reshape(layer_input.shape)
    )
    got = exchange(parts, "z_hi")
    summed = jnp.sum(got[:, : in_rows + text_rows].astype(jnp.float32), 0)
    back = jnp.concatenate([summed[:in_rows].astype(jnp.bfloat16), act_mean], 0)
    input_grad = inv_std * (
        normed_grad
        - jnp.mean(normed_grad, -1, keepdims=True)
        - standard * jnp.mean(normed_grad * standard, -1, keepdims=True)
    )
    input_grad = (input_grad + pool_grad[:, None, :] / patches).astype(jnp.bfloat16)
    back = spread(spread(pad_rows(back, 32), "z_hi"), "x_hi z_lo")
    back, input_grad = lax.optimization_barrier((back, input_grad))
    back = pair(back, "core")
    back = back.reshape(dp_count, 32, hidden_width)
    in_weight_grad = back[:, :in_rows].reshape(width_model, hidden_width)
    all_means = back[:, in_rows : in_rows + local_rows].reshape(-1, hidden_width)
    columns = got[:, in_rows + text_rows :, : 8 * column_width]
    columns = columns.reshape(8, local_rows, 8, column_width)
    columns = jnp.transpose(columns, (2, 0, 1, 3)).reshape(-1, column_width)
    out_weight_grad = jnp.einsum(
        "bf,bc->fc", all_means, columns, preferred_element_type=jnp.float32
    ).astype(jnp.bfloat16)

    text_acc = summed[in_rows:].reshape(text_count, width_model)
    paired_images = lax.dynamic_slice_in_dim(image_low, first_row, text_count, 0).astype(
        jnp.float32
    )
    text_dir = scale_value * (text_acc - weight_coef * paired_images)
    text_grad = unit_backward(text_dir, text_unit, text_inv)

    return (input_grad, in_weight_grad, out_weight_grad, rest_grad, text_grad)


def solution(mesh):
    in_specs = (
        P("dp", "mp", None),
        P("dp", "mp"),
        P("mp", None),
        P("dp", None),
        P(("dp", "mp"), None),
        P(),
        P(),
        P(),
    )
    out_specs = (
        P("dp", "mp", None),
        P(None, "mp"),
        P("mp", "dp"),
        P("dp", None),
        P(("dp", "mp"), None),
    )
    return jax.shard_map(body, mesh=mesh, in_specs=in_specs, out_specs=out_specs, check_vma=False)
```

```python
import functools
import math

import jax
import jax.numpy as jnp
from jax import lax
from jax.experimental import pallas as pl
from jax.experimental.pallas import tpu as pltpu
from jax.sharding import PartitionSpec as P

epsilon = 1e-06


def dp_index(x_hi, z_hi, z_lo, core):
    return 32 * x_hi + 4 * z_hi + 2 * z_lo + core


TWO, EIGHT = range(2), range(8)
GROUPS = {
    "core": [[dp_index(x, h, l, c) for c in TWO] for x in TWO for h in EIGHT for l in TWO],
    "x_hi": [[dp_index(x, h, l, c) for x in TWO] for h in EIGHT for l in TWO for c in TWO],
    "z": [[dp_index(x, h, l, c) for h in EIGHT for l in TWO] for x in TWO for c in TWO],
    "z_hi": [[dp_index(x, h, l, c) for h in EIGHT] for x in TWO for l in TWO for c in TWO],
    "x_hi z_lo": [[dp_index(x, h, l, c) for x in TWO for l in TWO] for h in EIGHT for c in TWO],
    "core x_hi": [[dp_index(x, h, l, c) for c in TWO for x in TWO] for h in EIGHT for l in TWO],
}


def norm_kernel(x_ref, normed_ref, total_ref):
    values = x_ref[0].astype(jnp.float32)
    centered = values - jnp.mean(values, -1, keepdims=True)
    inv_std = lax.rsqrt(jnp.mean(centered * centered, -1, keepdims=True) + epsilon)
    normed_ref[...] = (centered * inv_std).astype(jnp.bfloat16)
    total_ref[0] = jnp.sum(values, 0, keepdims=True)


def normalize(layer_input):
    rows, patches, width = layer_input.shape
    return pl.pallas_call(
        norm_kernel,
        grid=(rows,),
        in_specs=[pl.BlockSpec((1, patches, width), lambda i: (i, 0, 0))],
        out_specs=[
            pl.BlockSpec((patches, width), lambda i: (i, 0)),
            pl.BlockSpec((1, 1, width), lambda i: (i, 0, 0)),
        ],
        out_shape=[
            jax.ShapeDtypeStruct((rows * patches, width), jnp.bfloat16),
            jax.ShapeDtypeStruct((rows, 1, width), jnp.float32),
        ],
        compiler_params=pltpu.CompilerParams(vmem_limit_bytes=16 * 1024 * 1024),
    )(layer_input)


def hidden_kernel(
    rows, patches, x_ref, in_ref, out_ref, total_ref, slope_ref, act_ref, part_ref, sum_ref
):
    step = pl.program_id(0)
    hidden = jnp.dot(x_ref[...], in_ref[...], preferred_element_type=jnp.float32)
    root = math.sqrt(2.0 / math.pi)
    square = hidden * hidden
    tangent = jnp.tanh(root * (hidden + 0.044715 * square * hidden))
    half = 0.5 * (1.0 + tangent)
    slope_ref[...] = half + 0.5 * hidden * (1.0 - tangent * tangent) * root * (
        1.0 + 3.0 * 0.044715 * square
    )
    width = hidden.shape[1]
    sums = jnp.sum((hidden * half).reshape(-1, rows, patches, width), (0, 2))

    @pl.when(step == 0)
    def _():
        sum_ref[...] = sums

    @pl.when(step > 0)
    def _():
        sum_ref[...] += sums

    @pl.when(step == pl.num_programs(0) - 1)
    def _():
        act_mean = (sum_ref[...] * (1.0 / (8 * patches))).astype(jnp.bfloat16)
        act_ref[...] = act_mean
        part = jnp.dot(act_mean, out_ref[...], preferred_element_type=jnp.float32)
        part = part + total_ref[:, 0] * (1.0 / (8 * patches))
        part_ref[...] = jnp.broadcast_to(part[None], part_ref.shape)


def hidden_layer(flat, full_in, out_weight, totals, patches):
    tokens, width = flat.shape
    units = full_in.shape[1]
    rows = totals.shape[0]
    block = 2 * rows * patches
    return pl.pallas_call(
        functools.partial(hidden_kernel, rows, patches),
        grid=(tokens // block,),
        in_specs=[
            pl.BlockSpec((block, width), lambda i: (i, 0)),
            pl.BlockSpec((width, units), lambda i: (0, 0)),
            pl.BlockSpec((units, width), lambda i: (0, 0)),
            pl.BlockSpec((rows, 1, width), lambda i: (0, 0, 0)),
        ],
        out_specs=[
            pl.BlockSpec((block, units), lambda i: (i, 0)),
            pl.BlockSpec((rows, units), lambda i: (0, 0)),
            pl.BlockSpec((8, rows, width), lambda i: (0, 0, 0)),
        ],
        out_shape=[
            jax.ShapeDtypeStruct((tokens, units), jnp.float32),
            jax.ShapeDtypeStruct((rows, units), jnp.bfloat16),
            jax.ShapeDtypeStruct((8, rows, width), jnp.float32),
        ],
        scratch_shapes=[pltpu.VMEM((rows, units), jnp.float32)],
        compiler_params=pltpu.CompilerParams(vmem_limit_bytes=60 * 1024 * 1024),
    )(flat, full_in, out_weight, totals)


def unit_rows(values):
    norm_inv = lax.rsqrt(jnp.sum(values * values, -1, keepdims=True) + epsilon)
    return (values * norm_inv, norm_inv)


def unit_backward(grad_dir, unit_vals, norm_inv):
    return (grad_dir - unit_vals * jnp.sum(unit_vals * grad_dir, -1, keepdims=True)) * norm_inv


def exchange(blocks, axis):
    if axis in GROUPS:
        return lax.all_to_all(blocks, "dp", 0, 0, axis_index_groups=GROUPS[axis], tiled=True)
    return lax.all_to_all(blocks, axis, 0, 0, tiled=True)


def spread(block, axis):
    count = len(GROUPS[axis][0]) if axis in GROUPS else lax.axis_size(axis)
    return exchange(jnp.broadcast_to(block[None], (count,) + block.shape), axis)


def pair(block, axis):
    index = lax.axis_index("dp")
    first = (index % 2 if axis == "core" else index // 32) == 0
    other = lax.ppermute(block, "dp", [p for a, b in GROUPS[axis] for p in ((a, b), (b, a))])
    return jnp.stack([jnp.where(first, block, other), jnp.where(first, other, block)])


def sum_over(block, axis):
    return jnp.sum(spread(block, axis).astype(jnp.float32), 0)


def gather_z(block):
    return lax.all_gather(block, "dp", axis=0, axis_index_groups=GROUPS["z"], tiled=False)


def body(
    layer_input, in_weight, out_weight, image_rest, text_embed, log_scale, logit_bias, loss_scale
):
    local_rows, local_patches, width_model = layer_input.shape
    hidden_width = in_weight.shape[1]
    patches = local_patches * 8
    dp_count = 64
    in_rows = in_weight.shape[0]
    text_count = text_embed.shape[0]
    text_rows = text_count * width_model // hidden_width
    scale_value = jnp.exp(log_scale[0])
    image_count = local_rows + image_rest.shape[0]
    weight_coef = loss_scale[0] / (image_count * dp_count)

    normed, totals = normalize(layer_input)
    token_shape = (8, local_rows, local_patches, hidden_width)

    text_unit, text_inv = unit_rows(text_embed.astype(jnp.float32))
    text_low = text_unit.astype(jnp.bfloat16)
    in_weight, normed = lax.optimization_barrier((in_weight, normed))
    near = pair(in_weight, "x_hi").reshape(2 * in_rows, hidden_width)
    near = jnp.concatenate([near, text_low.reshape(text_rows, hidden_width)], 0)
    flat = lax.all_gather(normed, "mp", axis=0, tiled=True)
    both = gather_z(near)
    full_in = pair(both[:, : 2 * in_rows], "core").reshape(2, 16, 2, in_rows, hidden_width)
    full_in = jnp.transpose(full_in, (2, 1, 0, 3, 4)).reshape(width_model, hidden_width)
    texts = spread(both[:, 2 * in_rows :], "core x_hi")

    first_row = lax.axis_index("mp") * text_count
    zero_index = jnp.zeros((), jnp.int32)
    paired_texts = lax.dynamic_update_slice(
        jnp.zeros((image_count, width_model), jnp.float32),
        text_low.astype(jnp.float32),
        (first_row, zero_index),
    )
    slope, act_mean, part_pool = hidden_layer(flat, full_in, out_weight, totals, local_patches)
    part_pool, texts = lax.optimization_barrier((part_pool, texts))
    texts = jnp.transpose(texts.reshape(4, 8, 2, text_rows, hidden_width), (0, 2, 1, 3, 4))
    texts = texts.reshape(dp_count * text_count, width_model)
    pooled = jnp.sum(exchange(part_pool, "mp"), 0)
    images = jnp.concatenate([pooled, image_rest.astype(jnp.float32)], 0)
    image_unit, image_inv = unit_rows(images)
    image_low = image_unit.astype(jnp.bfloat16)
    logits = (
        scale_value * jnp.einsum("id,jd->ij", image_low, texts, preferred_element_type=jnp.float32)
        + logit_bias[0]
    )
    pair_weights = (weight_coef * jax.nn.sigmoid(logits)).astype(jnp.bfloat16)
    image_acc = jnp.dot(pair_weights, texts, preferred_element_type=jnp.float32)
    image_dir = scale_value * sum_over(
        (image_acc - weight_coef * paired_texts).astype(jnp.bfloat16), "mp"
    )
    image_grad = unit_backward(image_dir, image_unit, image_inv)
    pool_grad = image_grad[:local_rows]
    rest_grad = image_grad[local_rows:]
    pool_low = pool_grad.astype(jnp.bfloat16)
    row_grad = (
        jnp.einsum("bd,fd->bf", pool_low, out_weight, preferred_element_type=jnp.float32) / patches
    )
    hidden_grad = (
        (row_grad.reshape(1, local_rows, 1, hidden_width) * slope.reshape(token_shape))
        .astype(jnp.bfloat16)
        .reshape(-1, hidden_width)
    )

    text_part = jnp.einsum("ij,id->jd", pair_weights, image_low, preferred_element_type=jnp.float32)
    in_part = jnp.einsum("rd,rf->df", flat, hidden_grad, preferred_element_type=jnp.float32)
    index = lax.axis_index("dp")
    place = index % 2 * 4 + index // 32 * 2 + index // 2 % 2
    column_width = width_model // dp_count
    columns = pool_low.reshape(local_rows, 2, 8, 2, 2, column_width)
    columns = jnp.transpose(columns, (4, 1, 3, 2, 0, 5)).reshape(2, 4, 8, local_rows, column_width)
    columns = jnp.concatenate([columns] * 8, -1)
    columns = jnp.where(jnp.arange(8 * column_width) // column_width == place, columns, 0)
    columns = jnp.pad(columns, [(0, 0)] * 4 + [(0, hidden_width - columns.shape[-1])])
    parts = jnp.concatenate(
        [
            in_part.astype(jnp.bfloat16).reshape(2, 4, 8, in_rows, hidden_width),
            text_part.astype(jnp.bfloat16).reshape(2, 4, 8, text_rows, hidden_width),
            columns,
        ],
        3,
    )
    for axis in ("core", "x_hi z_lo"):
        got = exchange(parts, axis).astype(jnp.float32)
        parts = sum(got[k] for k in range(got.shape[0])).astype(jnp.bfloat16)
    normed_part = jnp.einsum(
        "rf,df->rd", hidden_grad, full_in, preferred_element_type=jnp.float32
    ).astype(jnp.bfloat16)
    normed_part, parts = lax.optimization_barrier((normed_part, parts))
    normed_grad = (
        lax.psum_scatter(normed_part, "mp", scatter_dimension=0, tiled=True)
        .astype(jnp.float32)
        .reshape(layer_input.shape)
    )
    got = exchange(parts, "z_hi")
    summed = jnp.sum(got[:, : in_rows + text_rows].astype(jnp.float32), 0)
    means = pair(act_mean, "core").reshape(2 * local_rows, hidden_width)
    back = jnp.concatenate([summed[:in_rows].astype(jnp.bfloat16), means], 0)
    normed_grad, again = lax.optimization_barrier((normed_grad, layer_input))
    inputs_f = again.astype(jnp.float32)
    centered = inputs_f - jnp.mean(inputs_f, -1, keepdims=True)
    inv_std = lax.rsqrt(jnp.mean(centered * centered, -1, keepdims=True) + epsilon)
    standard = centered * inv_std
    input_grad = inv_std * (
        normed_grad
        - jnp.mean(normed_grad, -1, keepdims=True)
        - standard * jnp.mean(normed_grad * standard, -1, keepdims=True)
    )
    input_grad = (input_grad + pool_grad[:, None, :] / patches).astype(jnp.bfloat16)
    back = spread(spread(back, "z_hi"), "x_hi z_lo")
    back, input_grad = lax.optimization_barrier((back, input_grad))
    back = back.reshape(dp_count // 2, -1, hidden_width)
    in_weight_grad = pair(back[:, :in_rows], "core").reshape(width_model, hidden_width)
    all_means = back[:, in_rows:].reshape(-1, hidden_width)
    columns = got[:, in_rows + text_rows :, : 8 * column_width]
    columns = columns.reshape(8, local_rows, 2, 4, column_width)
    columns = jnp.transpose(columns, (3, 0, 2, 1, 4)).reshape(-1, column_width)
    out_weight_grad = jnp.einsum(
        "bf,bc->fc", all_means, columns, preferred_element_type=jnp.float32
    ).astype(jnp.bfloat16)

    text_acc = summed[in_rows:].reshape(text_count, width_model)
    paired_images = lax.dynamic_slice_in_dim(image_low, first_row, text_count, 0).astype(
        jnp.float32
    )
    text_dir = scale_value * (text_acc - weight_coef * paired_images)
    text_grad = unit_backward(text_dir, text_unit, text_inv)

    return (input_grad, in_weight_grad, out_weight_grad, rest_grad, text_grad)


def solution(mesh):
    in_specs = (
        P("dp", "mp", None),
        P("dp", "mp"),
        P("mp", None),
        P("dp", None),
        P(("dp", "mp"), None),
        P(),
        P(),
        P(),
    )
    out_specs = (
        P("dp", "mp", None),
        P(None, "mp"),
        P("mp", "dp"),
        P("dp", None),
        P(("dp", "mp"), None),
    )
    return jax.shard_map(body, mesh=mesh, in_specs=in_specs, out_specs=out_specs, check_vma=False)
```

```python
import functools
import math

import jax
import jax.numpy as jnp
from jax import lax
from jax.experimental import pallas as pl
from jax.experimental.pallas import tpu as pltpu
from jax.sharding import PartitionSpec as P

epsilon = 1e-06


def dp_index(x_hi, z_hi, z_lo, core):
    return 32 * x_hi + 4 * z_hi + 2 * z_lo + core


TWO, EIGHT = range(2), range(8)
GROUPS = {
    "core": [[dp_index(x, h, l, c) for c in TWO] for x in TWO for h in EIGHT for l in TWO],
    "x_hi": [[dp_index(x, h, l, c) for x in TWO] for h in EIGHT for l in TWO for c in TWO],
    "z": [[dp_index(x, h, l, c) for h in EIGHT for l in TWO] for x in TWO for c in TWO],
    "z_hi": [[dp_index(x, h, l, c) for h in EIGHT] for x in TWO for l in TWO for c in TWO],
    "x_hi z_lo": [[dp_index(x, h, l, c) for x in TWO for l in TWO] for h in EIGHT for c in TWO],
    "core x_hi": [[dp_index(x, h, l, c) for c in TWO for x in TWO] for h in EIGHT for l in TWO],
}


def norm_kernel(x_ref, normed_ref, total_ref):
    values = x_ref[...].astype(jnp.float32)
    centered = values - jnp.mean(values, -1, keepdims=True)
    inv_std = lax.rsqrt(jnp.mean(centered * centered, -1, keepdims=True) + epsilon)
    normed_ref[...] = (centered * inv_std).astype(jnp.bfloat16).reshape(normed_ref.shape)
    total_ref[...] = jnp.sum(values, 1, keepdims=True)


def normalize(layer_input):
    rows, patches, width = layer_input.shape
    return pl.pallas_call(
        norm_kernel,
        grid=(2,),
        in_specs=[pl.BlockSpec((rows // 2, patches, width), lambda i: (i, 0, 0))],
        out_specs=[
            pl.BlockSpec((rows // 2 * patches, width), lambda i: (i, 0)),
            pl.BlockSpec((rows // 2, 1, width), lambda i: (i, 0, 0)),
        ],
        out_shape=[
            jax.ShapeDtypeStruct((rows * patches, width), jnp.bfloat16),
            jax.ShapeDtypeStruct((rows, 1, width), jnp.float32),
        ],
        compiler_params=pltpu.CompilerParams(vmem_limit_bytes=16 * 1024 * 1024),
    )(layer_input)


def hidden_kernel(
    rows, patches, x_ref, in_ref, out_ref, total_ref, slope_ref, act_ref, part_ref, sum_ref
):
    step = pl.program_id(0)
    hidden = jnp.dot(x_ref[...], in_ref[...], preferred_element_type=jnp.float32)
    root = math.sqrt(2.0 / math.pi)
    square = hidden * hidden
    tangent = jnp.tanh(root * (hidden + 0.044715 * square * hidden))
    half = 0.5 * (1.0 + tangent)
    slope_ref[...] = half + 0.5 * hidden * (1.0 - tangent * tangent) * root * (
        1.0 + 3.0 * 0.044715 * square
    )
    width = hidden.shape[1]
    sums = jnp.sum((hidden * half).reshape(-1, rows, patches, width), (0, 2))

    @pl.when(step == 0)
    def _():
        sum_ref[...] = sums

    @pl.when(step > 0)
    def _():
        sum_ref[...] += sums

    @pl.when(step == pl.num_programs(0) - 1)
    def _():
        act_mean = (sum_ref[...] * (1.0 / (8 * patches))).astype(jnp.bfloat16)
        act_ref[...] = act_mean
        part = jnp.dot(act_mean, out_ref[...], preferred_element_type=jnp.float32)
        part = part + total_ref[:, 0] * (1.0 / (8 * patches))
        part_ref[...] = jnp.broadcast_to(part[None], part_ref.shape)


def hidden_layer(flat, full_in, out_weight, totals, patches):
    tokens, width = flat.shape
    units = full_in.shape[1]
    rows = totals.shape[0]
    block = 2 * rows * patches
    return pl.pallas_call(
        functools.partial(hidden_kernel, rows, patches),
        grid=(tokens // block,),
        in_specs=[
            pl.BlockSpec((block, width), lambda i: (i, 0)),
            pl.BlockSpec((width, units), lambda i: (0, 0)),
            pl.BlockSpec((units, width), lambda i: (0, 0)),
            pl.BlockSpec((rows, 1, width), lambda i: (0, 0, 0)),
        ],
        out_specs=[
            pl.BlockSpec((block, units), lambda i: (i, 0)),
            pl.BlockSpec((rows, units), lambda i: (0, 0)),
            pl.BlockSpec((8, rows, width), lambda i: (0, 0, 0)),
        ],
        out_shape=[
            jax.ShapeDtypeStruct((tokens, units), jnp.float32),
            jax.ShapeDtypeStruct((rows, units), jnp.bfloat16),
            jax.ShapeDtypeStruct((8, rows, width), jnp.float32),
        ],
        scratch_shapes=[pltpu.VMEM((rows, units), jnp.float32)],
        compiler_params=pltpu.CompilerParams(vmem_limit_bytes=60 * 1024 * 1024),
    )(flat, full_in, out_weight, totals)


def unit_rows(values):
    norm_inv = lax.rsqrt(jnp.sum(values * values, -1, keepdims=True) + epsilon)
    return (values * norm_inv, norm_inv)


def unit_backward(grad_dir, unit_vals, norm_inv):
    return (grad_dir - unit_vals * jnp.sum(unit_vals * grad_dir, -1, keepdims=True)) * norm_inv


def exchange(blocks, axis):
    if axis in GROUPS:
        return lax.all_to_all(blocks, "dp", 0, 0, axis_index_groups=GROUPS[axis], tiled=True)
    return lax.all_to_all(blocks, axis, 0, 0, tiled=True)


def spread(block, axis):
    count = len(GROUPS[axis][0]) if axis in GROUPS else lax.axis_size(axis)
    return exchange(jnp.broadcast_to(block[None], (count,) + block.shape), axis)


def pair(block, axis):
    index = lax.axis_index("dp")
    first = (index % 2 if axis == "core" else index // 32) == 0
    other = lax.ppermute(block, "dp", [p for a, b in GROUPS[axis] for p in ((a, b), (b, a))])
    return jnp.stack([jnp.where(first, block, other), jnp.where(first, other, block)])


def sum_over(block, axis):
    return jnp.sum(spread(block, axis).astype(jnp.float32), 0)


def gather_z(block):
    return lax.all_gather(block, "dp", axis=0, axis_index_groups=GROUPS["z"], tiled=False)


def body(
    layer_input, in_weight, out_weight, image_rest, text_embed, log_scale, logit_bias, loss_scale
):
    local_rows, local_patches, width_model = layer_input.shape
    hidden_width = in_weight.shape[1]
    patches = local_patches * 8
    dp_count = 64
    in_rows = in_weight.shape[0]
    text_count = text_embed.shape[0]
    text_rows = text_count * width_model // hidden_width
    scale_value = jnp.exp(log_scale[0])
    image_count = local_rows + image_rest.shape[0]
    weight_coef = loss_scale[0] / (image_count * dp_count)

    normed, totals = normalize(layer_input)
    token_shape = (8, local_rows, local_patches, hidden_width)

    text_unit, text_inv = unit_rows(text_embed.astype(jnp.float32))
    text_low = text_unit.astype(jnp.bfloat16)
    in_weight, normed = lax.optimization_barrier((in_weight, normed))
    near = pair(in_weight, "x_hi").reshape(2 * in_rows, hidden_width)
    near = jnp.concatenate([near, text_low.reshape(text_rows, hidden_width)], 0)
    flat = lax.all_gather(normed, "mp", axis=0, tiled=True)
    both = gather_z(near)
    full_in = pair(both[:, : 2 * in_rows], "core").reshape(2, 16, 2, in_rows, hidden_width)
    full_in = jnp.transpose(full_in, (2, 1, 0, 3, 4)).reshape(width_model, hidden_width)
    texts = spread(both[:, 2 * in_rows :], "core x_hi")

    first_row = lax.axis_index("mp") * text_count
    zero_index = jnp.zeros((), jnp.int32)
    paired_texts = lax.dynamic_update_slice(
        jnp.zeros((image_count, width_model), jnp.float32),
        text_low.astype(jnp.float32),
        (first_row, zero_index),
    )
    slope, act_mean, part_pool = hidden_layer(flat, full_in, out_weight, totals, local_patches)
    part_pool, texts = lax.optimization_barrier((part_pool, texts))
    texts = jnp.transpose(texts.reshape(4, 8, 2, text_rows, hidden_width), (0, 2, 1, 3, 4))
    texts = texts.reshape(dp_count * text_count, width_model)
    pooled = jnp.sum(exchange(part_pool, "mp"), 0)
    images = jnp.concatenate([pooled, image_rest.astype(jnp.float32)], 0)
    image_unit, image_inv = unit_rows(images)
    image_low = image_unit.astype(jnp.bfloat16)
    logits = (
        scale_value * jnp.einsum("id,jd->ij", image_low, texts, preferred_element_type=jnp.float32)
        + logit_bias[0]
    )
    pair_weights = (weight_coef * jax.nn.sigmoid(logits)).astype(jnp.bfloat16)
    image_acc = jnp.dot(pair_weights, texts, preferred_element_type=jnp.float32)
    image_dir = scale_value * sum_over(
        (image_acc - weight_coef * paired_texts).astype(jnp.bfloat16), "mp"
    )
    image_grad = unit_backward(image_dir, image_unit, image_inv)
    pool_grad = image_grad[:local_rows]
    rest_grad = image_grad[local_rows:]
    pool_low = pool_grad.astype(jnp.bfloat16)
    row_grad = (
        jnp.einsum("bd,fd->bf", pool_low, out_weight, preferred_element_type=jnp.float32) / patches
    )
    hidden_grad = (
        (row_grad.reshape(1, local_rows, 1, hidden_width) * slope.reshape(token_shape))
        .astype(jnp.bfloat16)
        .reshape(-1, hidden_width)
    )

    text_part = jnp.einsum("ij,id->jd", pair_weights, image_low, preferred_element_type=jnp.float32)
    in_part = jnp.einsum("rd,rf->df", flat, hidden_grad, preferred_element_type=jnp.float32)
    index = lax.axis_index("dp")
    place = index % 2 * 4 + index // 32 * 2 + index // 2 % 2
    column_width = width_model // dp_count
    columns = pool_low.reshape(local_rows, 2, 8, 2, 2, column_width)
    columns = jnp.transpose(columns, (4, 1, 3, 2, 0, 5)).reshape(2, 4, 8, local_rows, column_width)
    columns = jnp.concatenate([columns] * 8, -1)
    columns = jnp.where(jnp.arange(8 * column_width) // column_width == place, columns, 0)
    columns = jnp.pad(columns, [(0, 0)] * 4 + [(0, hidden_width - columns.shape[-1])])
    parts = jnp.concatenate(
        [
            in_part.astype(jnp.bfloat16).reshape(2, 4, 8, in_rows, hidden_width),
            text_part.astype(jnp.bfloat16).reshape(2, 4, 8, text_rows, hidden_width),
            columns,
        ],
        3,
    )
    for axis in ("core", "x_hi z_lo"):
        got = exchange(parts, axis)
        parts = sum(got[k].astype(jnp.float32) for k in range(got.shape[0])).astype(jnp.bfloat16)
    normed_part = jnp.einsum(
        "rf,df->rd", hidden_grad, full_in, preferred_element_type=jnp.float32
    ).astype(jnp.bfloat16)
    normed_part, parts = lax.optimization_barrier((normed_part, parts))
    normed_grad = (
        lax.psum_scatter(normed_part, "mp", scatter_dimension=0, tiled=True)
        .astype(jnp.float32)
        .reshape(layer_input.shape)
    )
    got = exchange(parts, "z_hi")
    summed = jnp.sum(got[:, : in_rows + text_rows].astype(jnp.float32), 0)
    means = pair(act_mean, "core").reshape(2 * local_rows, hidden_width)
    back = jnp.concatenate([summed[:in_rows].astype(jnp.bfloat16), means], 0)
    normed_grad, again = lax.optimization_barrier((normed_grad, layer_input))
    inputs_f = again.astype(jnp.float32)
    centered = inputs_f - jnp.mean(inputs_f, -1, keepdims=True)
    inv_std = lax.rsqrt(jnp.mean(centered * centered, -1, keepdims=True) + epsilon)
    standard = centered * inv_std
    input_grad = inv_std * (
        normed_grad
        - jnp.mean(normed_grad, -1, keepdims=True)
        - standard * jnp.mean(normed_grad * standard, -1, keepdims=True)
    )
    input_grad = (input_grad + pool_grad[:, None, :] / patches).astype(jnp.bfloat16)
    back = spread(spread(back, "z_hi"), "x_hi z_lo")
    back, input_grad = lax.optimization_barrier((back, input_grad))
    back = back.reshape(dp_count // 2, -1, hidden_width)
    in_weight_grad = pair(back[:, :in_rows], "core").reshape(width_model, hidden_width)
    all_means = back[:, in_rows:].reshape(-1, hidden_width)
    columns = got[:, in_rows + text_rows :, : 8 * column_width]
    columns = columns.reshape(8, local_rows, 2, 4, column_width)
    columns = jnp.transpose(columns, (3, 0, 2, 1, 4)).reshape(-1, column_width)
    out_weight_grad = jnp.einsum(
        "bf,bc->fc", all_means, columns, preferred_element_type=jnp.float32
    ).astype(jnp.bfloat16)

    text_acc = summed[in_rows:].reshape(text_count, width_model)
    paired_images = lax.dynamic_slice_in_dim(image_low, first_row, text_count, 0).astype(
        jnp.float32
    )
    text_dir = scale_value * (text_acc - weight_coef * paired_images)
    text_grad = unit_backward(text_dir, text_unit, text_inv)

    return (input_grad, in_weight_grad, out_weight_grad, rest_grad, text_grad)


def solution(mesh):
    in_specs = (
        P("dp", "mp", None),
        P("dp", "mp"),
        P("mp", None),
        P("dp", None),
        P(("dp", "mp"), None),
        P(),
        P(),
        P(),
    )
    out_specs = (
        P("dp", "mp", None),
        P(None, "mp"),
        P("mp", "dp"),
        P("dp", None),
        P(("dp", "mp"), None),
    )
    return jax.shard_map(body, mesh=mesh, in_specs=in_specs, out_specs=out_specs, check_vma=False)
```

```python
import functools
import math

import jax
import jax.numpy as jnp
from jax import lax
from jax.experimental import pallas as pl
from jax.experimental.pallas import tpu as pltpu
from jax.sharding import PartitionSpec as P

epsilon = 1e-06


def dp_index(x_hi, z_hi, z_lo, core):
    return 32 * x_hi + 4 * z_hi + 2 * z_lo + core


TWO, EIGHT = range(2), range(8)
GROUPS = {
    "core": [[dp_index(x, h, l, c) for c in TWO] for x in TWO for h in EIGHT for l in TWO],
    "x_hi": [[dp_index(x, h, l, c) for x in TWO] for h in EIGHT for l in TWO for c in TWO],
    "z": [[dp_index(x, h, l, c) for h in EIGHT for l in TWO] for x in TWO for c in TWO],
    "z_hi": [[dp_index(x, h, l, c) for h in EIGHT] for x in TWO for l in TWO for c in TWO],
    "x_hi z_lo": [[dp_index(x, h, l, c) for x in TWO for l in TWO] for h in EIGHT for c in TWO],
    "core x_hi": [[dp_index(x, h, l, c) for c in TWO for x in TWO] for h in EIGHT for l in TWO],
}


def norm_kernel(x_ref, normed_ref, total_ref):
    values = x_ref[...].astype(jnp.float32)
    centered = values - jnp.mean(values, -1, keepdims=True)
    inv_std = lax.rsqrt(jnp.mean(centered * centered, -1, keepdims=True) + epsilon)
    normed_ref[...] = (centered * inv_std).astype(jnp.bfloat16).reshape(normed_ref.shape)
    total_ref[...] = jnp.sum(values, 1, keepdims=True)


def normalize(layer_input):
    rows, patches, width = layer_input.shape
    return pl.pallas_call(
        norm_kernel,
        grid=(2,),
        in_specs=[pl.BlockSpec((rows // 2, patches, width), lambda i: (i, 0, 0))],
        out_specs=[
            pl.BlockSpec((rows // 2 * patches, width), lambda i: (i, 0)),
            pl.BlockSpec((rows // 2, 1, width), lambda i: (i, 0, 0)),
        ],
        out_shape=[
            jax.ShapeDtypeStruct((rows * patches, width), jnp.bfloat16),
            jax.ShapeDtypeStruct((rows, 1, width), jnp.float32),
        ],
        compiler_params=pltpu.CompilerParams(vmem_limit_bytes=16 * 1024 * 1024),
    )(layer_input)


def hidden_kernel(
    rows, patches, x_ref, in_ref, out_ref, total_ref, slope_ref, act_ref, part_ref, sum_ref
):
    step = pl.program_id(0)
    hidden = jnp.dot(x_ref[...], in_ref[...], preferred_element_type=jnp.float32)
    root = math.sqrt(2.0 / math.pi)
    square = hidden * hidden
    tangent = jnp.tanh(root * (hidden + 0.044715 * square * hidden))
    half = 0.5 * (1.0 + tangent)
    slope_ref[...] = half + 0.5 * hidden * (1.0 - tangent * tangent) * root * (
        1.0 + 3.0 * 0.044715 * square
    )
    width = hidden.shape[1]
    sums = jnp.sum((hidden * half).reshape(-1, rows, patches, width), (0, 2))

    @pl.when(step == 0)
    def _():
        sum_ref[...] = sums

    @pl.when(step > 0)
    def _():
        sum_ref[...] += sums

    @pl.when(step == pl.num_programs(0) - 1)
    def _():
        act_mean = (sum_ref[...] * (1.0 / (8 * patches))).astype(jnp.bfloat16)
        act_ref[...] = act_mean
        part = jnp.dot(act_mean, out_ref[...], preferred_element_type=jnp.float32)
        part = part + total_ref[:, 0] * (1.0 / (8 * patches))
        part_ref[...] = jnp.broadcast_to(part.astype(jnp.bfloat16)[None], part_ref.shape)


def hidden_layer(flat, full_in, out_weight, totals, patches):
    tokens, width = flat.shape
    units = full_in.shape[1]
    rows = totals.shape[0]
    block = 4 * rows * patches
    return pl.pallas_call(
        functools.partial(hidden_kernel, rows, patches),
        grid=(tokens // block,),
        in_specs=[
            pl.BlockSpec((block, width), lambda i: (i, 0)),
            pl.BlockSpec((width, units), lambda i: (0, 0)),
            pl.BlockSpec((units, width), lambda i: (0, 0)),
            pl.BlockSpec((rows, 1, width), lambda i: (0, 0, 0)),
        ],
        out_specs=[
            pl.BlockSpec((block, units), lambda i: (i, 0)),
            pl.BlockSpec((rows, units), lambda i: (0, 0)),
            pl.BlockSpec((8, rows, width), lambda i: (0, 0, 0)),
        ],
        out_shape=[
            jax.ShapeDtypeStruct((tokens, units), jnp.float32),
            jax.ShapeDtypeStruct((rows, units), jnp.bfloat16),
            jax.ShapeDtypeStruct((8, rows, width), jnp.bfloat16),
        ],
        scratch_shapes=[pltpu.VMEM((rows, units), jnp.float32)],
        compiler_params=pltpu.CompilerParams(vmem_limit_bytes=60 * 1024 * 1024),
    )(flat, full_in, out_weight, totals)


def unit_rows(values):
    norm_inv = lax.rsqrt(jnp.sum(values * values, -1, keepdims=True) + epsilon)
    return (values * norm_inv, norm_inv)


def unit_backward(grad_dir, unit_vals, norm_inv):
    return (grad_dir - unit_vals * jnp.sum(unit_vals * grad_dir, -1, keepdims=True)) * norm_inv


def exchange(blocks, axis):
    if axis in GROUPS:
        return lax.all_to_all(blocks, "dp", 0, 0, axis_index_groups=GROUPS[axis], tiled=True)
    return lax.all_to_all(blocks, axis, 0, 0, tiled=True)


def spread(block, axis):
    count = len(GROUPS[axis][0]) if axis in GROUPS else lax.axis_size(axis)
    return exchange(jnp.broadcast_to(block[None], (count,) + block.shape), axis)


def pair(block, axis):
    index = lax.axis_index("dp")
    first = (index % 2 if axis == "core" else index // 32) == 0
    other = lax.ppermute(block, "dp", [p for a, b in GROUPS[axis] for p in ((a, b), (b, a))])
    return jnp.stack([jnp.where(first, block, other), jnp.where(first, other, block)])


def sum_over(block, axis):
    return jnp.sum(spread(block, axis).astype(jnp.float32), 0)


def gather_z(block):
    return lax.all_gather(block, "dp", axis=0, axis_index_groups=GROUPS["z"], tiled=False)


def body(
    layer_input, in_weight, out_weight, image_rest, text_embed, log_scale, logit_bias, loss_scale
):
    local_rows, local_patches, width_model = layer_input.shape
    hidden_width = in_weight.shape[1]
    patches = local_patches * 8
    dp_count = 64
    in_rows = in_weight.shape[0]
    text_count = text_embed.shape[0]
    text_rows = text_count * width_model // hidden_width
    scale_value = jnp.exp(log_scale[0])
    image_count = local_rows + image_rest.shape[0]
    weight_coef = loss_scale[0] / (image_count * dp_count)

    normed, totals = normalize(layer_input)
    token_shape = (8, local_rows, local_patches, hidden_width)

    text_unit, text_inv = unit_rows(text_embed.astype(jnp.float32))
    text_low = text_unit.astype(jnp.bfloat16)
    in_weight, normed = lax.optimization_barrier((in_weight, normed))
    near = pair(in_weight, "x_hi").reshape(2 * in_rows, hidden_width)
    near = jnp.concatenate([near, text_low.reshape(text_rows, hidden_width)], 0)
    flat = lax.all_gather(normed, "mp", axis=0, tiled=True)
    both = gather_z(near)
    full_in = pair(both[:, : 2 * in_rows], "core").reshape(2, 16, 2, in_rows, hidden_width)
    full_in = jnp.transpose(full_in, (2, 1, 0, 3, 4)).reshape(width_model, hidden_width)
    texts = spread(both[:, 2 * in_rows :], "core x_hi")

    first_row = lax.axis_index("mp") * text_count
    zero_index = jnp.zeros((), jnp.int32)
    paired_texts = lax.dynamic_update_slice(
        jnp.zeros((image_count, width_model), jnp.float32),
        text_low.astype(jnp.float32),
        (first_row, zero_index),
    )
    slope, act_mean, part_pool = hidden_layer(flat, full_in, out_weight, totals, local_patches)
    part_pool, texts = lax.optimization_barrier((part_pool, texts))
    texts = jnp.transpose(texts.reshape(4, 8, 2, text_rows, hidden_width), (0, 2, 1, 3, 4))
    texts = texts.reshape(dp_count * text_count, width_model)
    pooled = jnp.sum(exchange(part_pool, "mp").astype(jnp.float32), 0)
    images = jnp.concatenate([pooled, image_rest.astype(jnp.float32)], 0)
    image_unit, image_inv = unit_rows(images)
    image_low = image_unit.astype(jnp.bfloat16)
    logits = (
        scale_value * jnp.einsum("id,jd->ij", image_low, texts, preferred_element_type=jnp.float32)
        + logit_bias[0]
    )
    pair_weights = (weight_coef * jax.nn.sigmoid(logits)).astype(jnp.bfloat16)
    image_acc = jnp.dot(pair_weights, texts, preferred_element_type=jnp.float32)
    image_dir = scale_value * sum_over(
        (image_acc - weight_coef * paired_texts).astype(jnp.bfloat16), "mp"
    )
    image_grad = unit_backward(image_dir, image_unit, image_inv)
    pool_grad = image_grad[:local_rows]
    rest_grad = image_grad[local_rows:]
    pool_low = pool_grad.astype(jnp.bfloat16)
    row_grad = (
        jnp.einsum("bd,fd->bf", pool_low, out_weight, preferred_element_type=jnp.float32) / patches
    )
    hidden_grad = (
        (row_grad.reshape(1, local_rows, 1, hidden_width) * slope.reshape(token_shape))
        .astype(jnp.bfloat16)
        .reshape(-1, hidden_width)
    )

    text_part = jnp.einsum("ij,id->jd", pair_weights, image_low, preferred_element_type=jnp.float32)
    in_part = jnp.einsum("rd,rf->df", flat, hidden_grad, preferred_element_type=jnp.float32)
    index = lax.axis_index("dp")
    place = index % 2 * 4 + index // 32 * 2 + index // 2 % 2
    column_width = width_model // dp_count
    columns = pool_low.reshape(local_rows, 2, 8, 2, 2, column_width)
    columns = jnp.transpose(columns, (4, 1, 3, 2, 0, 5)).reshape(2, 4, 8, local_rows, column_width)
    columns = jnp.concatenate([columns] * 8, -1)
    columns = jnp.where(jnp.arange(8 * column_width) // column_width == place, columns, 0)
    columns = jnp.pad(columns, [(0, 0)] * 4 + [(0, hidden_width - columns.shape[-1])])
    parts = jnp.concatenate(
        [
            in_part.astype(jnp.bfloat16).reshape(2, 4, 8, in_rows, hidden_width),
            text_part.astype(jnp.bfloat16).reshape(2, 4, 8, text_rows, hidden_width),
            columns,
        ],
        3,
    )
    for axis in ("core", "x_hi z_lo"):
        got = exchange(parts, axis)
        parts = sum(got[k].astype(jnp.float32) for k in range(got.shape[0])).astype(jnp.bfloat16)
    normed_part = jnp.einsum(
        "rf,df->rd", hidden_grad, full_in, preferred_element_type=jnp.float32
    ).astype(jnp.bfloat16)
    normed_part, parts = lax.optimization_barrier((normed_part, parts))
    normed_grad = (
        lax.psum_scatter(normed_part, "mp", scatter_dimension=0, tiled=True)
        .astype(jnp.float32)
        .reshape(layer_input.shape)
    )
    got = exchange(parts, "z_hi")
    summed = jnp.sum(got[:, : in_rows + text_rows].astype(jnp.float32), 0)
    means = pair(act_mean, "core").reshape(2 * local_rows, hidden_width)
    back = jnp.concatenate([summed[:in_rows].astype(jnp.bfloat16), means], 0)
    normed_grad, again = lax.optimization_barrier((normed_grad, layer_input))
    inputs_f = again.astype(jnp.float32)
    centered = inputs_f - jnp.mean(inputs_f, -1, keepdims=True)
    inv_std = lax.rsqrt(jnp.mean(centered * centered, -1, keepdims=True) + epsilon)
    standard = centered * inv_std
    input_grad = inv_std * (
        normed_grad
        - jnp.mean(normed_grad, -1, keepdims=True)
        - standard * jnp.mean(normed_grad * standard, -1, keepdims=True)
    )
    input_grad = (input_grad + pool_grad[:, None, :] / patches).astype(jnp.bfloat16)
    back = spread(spread(back, "z_hi"), "x_hi z_lo")
    back, input_grad = lax.optimization_barrier((back, input_grad))
    back = back.reshape(dp_count // 2, -1, hidden_width)
    in_weight_grad = pair(back[:, :in_rows], "core").reshape(width_model, hidden_width)
    all_means = back[:, in_rows:].reshape(-1, hidden_width)
    columns = got[:, in_rows + text_rows :, : 8 * column_width]
    columns = columns.reshape(8, local_rows, 2, 4, column_width)
    columns = jnp.transpose(columns, (3, 0, 2, 1, 4)).reshape(-1, column_width)
    out_weight_grad = jnp.einsum(
        "bf,bc->fc", all_means, columns, preferred_element_type=jnp.float32
    ).astype(jnp.bfloat16)

    text_acc = summed[in_rows:].reshape(text_count, width_model)
    paired_images = lax.dynamic_slice_in_dim(image_low, first_row, text_count, 0).astype(
        jnp.float32
    )
    text_dir = scale_value * (text_acc - weight_coef * paired_images)
    text_grad = unit_backward(text_dir, text_unit, text_inv)

    return (input_grad, in_weight_grad, out_weight_grad, rest_grad, text_grad)


def solution(mesh):
    in_specs = (
        P("dp", "mp", None),
        P("dp", "mp"),
        P("mp", None),
        P("dp", None),
        P(("dp", "mp"), None),
        P(),
        P(),
        P(),
    )
    out_specs = (
        P("dp", "mp", None),
        P(None, "mp"),
        P("mp", "dp"),
        P("dp", None),
        P(("dp", "mp"), None),
    )
    return jax.shard_map(body, mesh=mesh, in_specs=in_specs, out_specs=out_specs, check_vma=False)
```

```python
import functools
import math

import jax
import jax.numpy as jnp
from jax import lax
from jax.experimental import pallas as pl
from jax.experimental.pallas import tpu as pltpu
from jax.sharding import PartitionSpec as P

epsilon = 1e-06


def dp_index(x_hi, z_hi, z_lo, core):
    return 32 * x_hi + 4 * z_hi + 2 * z_lo + core


TWO, EIGHT = range(2), range(8)
GROUPS = {
    "core": [[dp_index(x, h, l, c) for c in TWO] for x in TWO for h in EIGHT for l in TWO],
    "x_hi": [[dp_index(x, h, l, c) for x in TWO] for h in EIGHT for l in TWO for c in TWO],
    "z": [[dp_index(x, h, l, c) for h in EIGHT for l in TWO] for x in TWO for c in TWO],
    "z_hi": [[dp_index(x, h, l, c) for h in EIGHT] for x in TWO for l in TWO for c in TWO],
    "x_hi z_lo": [[dp_index(x, h, l, c) for x in TWO for l in TWO] for h in EIGHT for c in TWO],
    "core x_hi": [[dp_index(x, h, l, c) for c in TWO for x in TWO] for h in EIGHT for l in TWO],
}


def norm_kernel(x_ref, normed_ref, total_ref):
    values = x_ref[...].astype(jnp.float32)
    centered = values - jnp.mean(values, -1, keepdims=True)
    inv_std = lax.rsqrt(jnp.mean(centered * centered, -1, keepdims=True) + epsilon)
    normed_ref[...] = (centered * inv_std).astype(jnp.bfloat16).reshape(normed_ref.shape)
    total_ref[...] = jnp.sum(values, 1, keepdims=True)


def normalize(layer_input):
    rows, patches, width = layer_input.shape
    return pl.pallas_call(
        norm_kernel,
        grid=(2,),
        in_specs=[pl.BlockSpec((rows // 2, patches, width), lambda i: (i, 0, 0))],
        out_specs=[
            pl.BlockSpec((rows // 2 * patches, width), lambda i: (i, 0)),
            pl.BlockSpec((rows // 2, 1, width), lambda i: (i, 0, 0)),
        ],
        out_shape=[
            jax.ShapeDtypeStruct((rows * patches, width), jnp.bfloat16),
            jax.ShapeDtypeStruct((rows, 1, width), jnp.float32),
        ],
        compiler_params=pltpu.CompilerParams(vmem_limit_bytes=16 * 1024 * 1024),
    )(layer_input)


def hidden_kernel(
    rows, patches, x_ref, in_ref, out_ref, total_ref, slope_ref, act_ref, part_ref, sum_ref
):
    step = pl.program_id(0)
    hidden = jnp.dot(x_ref[...], in_ref[...], preferred_element_type=jnp.float32)
    root = math.sqrt(2.0 / math.pi)
    square = hidden * hidden
    tangent = jnp.tanh(root * (hidden + 0.044715 * square * hidden))
    half = 0.5 * (1.0 + tangent)
    slope_ref[...] = half + 0.5 * hidden * (1.0 - tangent * tangent) * root * (
        1.0 + 3.0 * 0.044715 * square
    )
    width = hidden.shape[1]
    sums = jnp.sum((hidden * half).reshape(-1, rows, patches, width), (0, 2))

    @pl.when(step == 0)
    def _():
        sum_ref[...] = sums

    @pl.when(step > 0)
    def _():
        sum_ref[...] += sums

    @pl.when(step == pl.num_programs(0) - 1)
    def _():
        act_mean = (sum_ref[...] * (1.0 / (8 * patches))).astype(jnp.bfloat16)
        act_ref[...] = act_mean
        part = jnp.dot(act_mean, out_ref[...], preferred_element_type=jnp.float32)
        part = part + total_ref[:, 0] * (1.0 / (8 * patches))
        part_ref[...] = jnp.broadcast_to(part.astype(jnp.bfloat16)[None], part_ref.shape)


def hidden_layer(flat, full_in, out_weight, totals, patches):
    tokens, width = flat.shape
    units = full_in.shape[1]
    rows = totals.shape[0]
    block = 4 * rows * patches
    return pl.pallas_call(
        functools.partial(hidden_kernel, rows, patches),
        grid=(tokens // block,),
        in_specs=[
            pl.BlockSpec((block, width), lambda i: (i, 0)),
            pl.BlockSpec((width, units), lambda i: (0, 0)),
            pl.BlockSpec((units, width), lambda i: (0, 0)),
            pl.BlockSpec((rows, 1, width), lambda i: (0, 0, 0)),
        ],
        out_specs=[
            pl.BlockSpec((block, units), lambda i: (i, 0)),
            pl.BlockSpec((rows, units), lambda i: (0, 0)),
            pl.BlockSpec((8, rows, width), lambda i: (0, 0, 0)),
        ],
        out_shape=[
            jax.ShapeDtypeStruct((tokens, units), jnp.float32),
            jax.ShapeDtypeStruct((rows, units), jnp.bfloat16),
            jax.ShapeDtypeStruct((8, rows, width), jnp.bfloat16),
        ],
        scratch_shapes=[pltpu.VMEM((rows, units), jnp.float32)],
        compiler_params=pltpu.CompilerParams(vmem_limit_bytes=60 * 1024 * 1024),
    )(flat, full_in, out_weight, totals)


def unit_rows(values):
    norm_inv = lax.rsqrt(jnp.sum(values * values, -1, keepdims=True) + epsilon)
    return (values * norm_inv, norm_inv)


def unit_backward(grad_dir, unit_vals, norm_inv):
    return (grad_dir - unit_vals * jnp.sum(unit_vals * grad_dir, -1, keepdims=True)) * norm_inv


def exchange(blocks, axis):
    if axis in GROUPS:
        return lax.all_to_all(blocks, "dp", 0, 0, axis_index_groups=GROUPS[axis], tiled=True)
    return lax.all_to_all(blocks, axis, 0, 0, tiled=True)


def spread(block, axis):
    count = len(GROUPS[axis][0]) if axis in GROUPS else lax.axis_size(axis)
    return exchange(jnp.broadcast_to(block[None], (count,) + block.shape), axis)


def pair(block, axis):
    index = lax.axis_index("dp")
    first = (index % 2 if axis == "core" else index // 32) == 0
    other = lax.ppermute(block, "dp", [p for a, b in GROUPS[axis] for p in ((a, b), (b, a))])
    return jnp.stack([jnp.where(first, block, other), jnp.where(first, other, block)])


def sum_over(block, axis):
    return jnp.sum(spread(block, axis).astype(jnp.float32), 0)


def gather_z(block):
    return lax.all_gather(block, "dp", axis=0, axis_index_groups=GROUPS["z"], tiled=False)


def body(
    layer_input, in_weight, out_weight, image_rest, text_embed, log_scale, logit_bias, loss_scale
):
    local_rows, local_patches, width_model = layer_input.shape
    hidden_width = in_weight.shape[1]
    patches = local_patches * 8
    dp_count = 64
    in_rows = in_weight.shape[0]
    text_count = text_embed.shape[0]
    text_rows = text_count * width_model // hidden_width
    scale_value = jnp.exp(log_scale[0])
    image_count = local_rows + image_rest.shape[0]
    weight_coef = loss_scale[0] / (image_count * dp_count)

    normed, totals = normalize(layer_input)
    token_shape = (8, local_rows, local_patches, hidden_width)

    text_unit, text_inv = unit_rows(text_embed.astype(jnp.float32))
    text_low = text_unit.astype(jnp.bfloat16)
    in_weight, normed = lax.optimization_barrier((in_weight, normed))
    near = pair(in_weight, "x_hi").reshape(2 * in_rows, hidden_width)
    near = jnp.concatenate([near, text_low.reshape(text_rows, hidden_width)], 0)
    flat = lax.all_gather(normed, "mp", axis=0, tiled=True)
    both = gather_z(near)
    full_in = pair(both[:, : 2 * in_rows], "core").reshape(2, 16, 2, in_rows, hidden_width)
    full_in = jnp.transpose(full_in, (2, 1, 0, 3, 4)).reshape(width_model, hidden_width)
    texts = spread(both[:, 2 * in_rows :], "x_hi")

    first_row = lax.axis_index("mp") * text_count
    zero_index = jnp.zeros((), jnp.int32)
    paired_texts = lax.dynamic_update_slice(
        jnp.zeros((image_count, width_model), jnp.float32),
        text_low.astype(jnp.float32),
        (first_row, zero_index),
    )
    slope, act_mean, part_pool = hidden_layer(flat, full_in, out_weight, totals, local_patches)
    part_pool, texts = lax.optimization_barrier((part_pool, texts))
    texts = pair(texts, "core")
    texts = jnp.transpose(texts.reshape(4, 8, 2, text_rows, hidden_width), (0, 2, 1, 3, 4))
    texts = texts.reshape(dp_count * text_count, width_model)
    pooled = jnp.sum(exchange(part_pool, "mp").astype(jnp.float32), 0)
    images = jnp.concatenate([pooled, image_rest.astype(jnp.float32)], 0)
    image_unit, image_inv = unit_rows(images)
    image_low = image_unit.astype(jnp.bfloat16)
    logits = (
        scale_value * jnp.einsum("id,jd->ij", image_low, texts, preferred_element_type=jnp.float32)
        + logit_bias[0]
    )
    pair_weights = (weight_coef * jax.nn.sigmoid(logits)).astype(jnp.bfloat16)
    image_acc = jnp.dot(pair_weights, texts, preferred_element_type=jnp.float32)
    image_dir = scale_value * sum_over(
        (image_acc - weight_coef * paired_texts).astype(jnp.bfloat16), "mp"
    )
    image_grad = unit_backward(image_dir, image_unit, image_inv)
    pool_grad = image_grad[:local_rows]
    rest_grad = image_grad[local_rows:]
    pool_low = pool_grad.astype(jnp.bfloat16)
    row_grad = (
        jnp.einsum("bd,fd->bf", pool_low, out_weight, preferred_element_type=jnp.float32) / patches
    )
    hidden_grad = (
        (row_grad.reshape(1, local_rows, 1, hidden_width) * slope.reshape(token_shape))
        .astype(jnp.bfloat16)
        .reshape(-1, hidden_width)
    )

    text_part = jnp.einsum("ij,id->jd", pair_weights, image_low, preferred_element_type=jnp.float32)
    in_part = jnp.einsum("rd,rf->df", flat, hidden_grad, preferred_element_type=jnp.float32)
    index = lax.axis_index("dp")
    place = index % 2 * 4 + index // 32 * 2 + index // 2 % 2
    column_width = width_model // dp_count
    columns = pool_low.reshape(local_rows, 2, 8, 2, 2, column_width)
    columns = jnp.transpose(columns, (4, 1, 3, 2, 0, 5)).reshape(2, 4, 8, local_rows, column_width)
    columns = jnp.concatenate([columns] * 8, -1)
    columns = jnp.where(jnp.arange(8 * column_width) // column_width == place, columns, 0)
    columns = jnp.pad(columns, [(0, 0)] * 4 + [(0, hidden_width - columns.shape[-1])])
    parts = jnp.concatenate(
        [
            in_part.astype(jnp.bfloat16).reshape(2, 4, 8, in_rows, hidden_width),
            text_part.astype(jnp.bfloat16).reshape(2, 4, 8, text_rows, hidden_width),
            columns,
        ],
        3,
    )
    for axis in ("core", "x_hi z_lo"):
        got = exchange(parts, axis)
        parts = sum(got[k].astype(jnp.float32) for k in range(got.shape[0])).astype(jnp.bfloat16)
    normed_part = jnp.einsum(
        "rf,df->rd", hidden_grad, full_in, preferred_element_type=jnp.float32
    ).astype(jnp.bfloat16)
    normed_part, parts = lax.optimization_barrier((normed_part, parts))
    normed_grad = (
        lax.psum_scatter(normed_part, "mp", scatter_dimension=0, tiled=True)
        .astype(jnp.float32)
        .reshape(layer_input.shape)
    )
    got = exchange(parts, "z_hi")
    summed = jnp.sum(got[:, : in_rows + text_rows].astype(jnp.float32), 0)
    means = pair(act_mean, "core").reshape(2 * local_rows, hidden_width)
    back = jnp.concatenate([summed[:in_rows].astype(jnp.bfloat16), means], 0)
    normed_grad, again = lax.optimization_barrier((normed_grad, layer_input))
    inputs_f = again.astype(jnp.float32)
    centered = inputs_f - jnp.mean(inputs_f, -1, keepdims=True)
    inv_std = lax.rsqrt(jnp.mean(centered * centered, -1, keepdims=True) + epsilon)
    standard = centered * inv_std
    input_grad = inv_std * (
        normed_grad
        - jnp.mean(normed_grad, -1, keepdims=True)
        - standard * jnp.mean(normed_grad * standard, -1, keepdims=True)
    )
    input_grad = (input_grad + pool_grad[:, None, :] / patches).astype(jnp.bfloat16)
    back = spread(spread(back, "z_hi"), "x_hi z_lo")
    back, input_grad = lax.optimization_barrier((back, input_grad))
    back = back.reshape(dp_count // 2, -1, hidden_width)
    in_weight_grad = pair(back[:, :in_rows], "core").reshape(width_model, hidden_width)
    all_means = back[:, in_rows:].reshape(-1, hidden_width)
    columns = got[:, in_rows + text_rows :, : 8 * column_width]
    columns = columns.reshape(8, local_rows, 2, 4, column_width)
    columns = jnp.transpose(columns, (3, 0, 2, 1, 4)).reshape(-1, column_width)
    out_weight_grad = jnp.einsum(
        "bf,bc->fc", all_means, columns, preferred_element_type=jnp.float32
    ).astype(jnp.bfloat16)

    text_acc = summed[in_rows:].reshape(text_count, width_model)
    paired_images = lax.dynamic_slice_in_dim(image_low, first_row, text_count, 0).astype(
        jnp.float32
    )
    text_dir = scale_value * (text_acc - weight_coef * paired_images)
    text_grad = unit_backward(text_dir, text_unit, text_inv)

    return (input_grad, in_weight_grad, out_weight_grad, rest_grad, text_grad)


def solution(mesh):
    in_specs = (
        P("dp", "mp", None),
        P("dp", "mp"),
        P("mp", None),
        P("dp", None),
        P(("dp", "mp"), None),
        P(),
        P(),
        P(),
    )
    out_specs = (
        P("dp", "mp", None),
        P(None, "mp"),
        P("mp", "dp"),
        P("dp", None),
        P(("dp", "mp"), None),
    )
    return jax.shard_map(body, mesh=mesh, in_specs=in_specs, out_specs=out_specs, check_vma=False)
```

```python
import functools
import math

import jax
import jax.numpy as jnp
from jax import lax
from jax.experimental import pallas as pl
from jax.experimental.pallas import tpu as pltpu
from jax.sharding import PartitionSpec as P

epsilon = 1e-06


def dp_index(x_hi, z_hi, z_lo, core):
    return 32 * x_hi + 4 * z_hi + 2 * z_lo + core


TWO, EIGHT = range(2), range(8)
GROUPS = {
    "core": [[dp_index(x, h, l, c) for c in TWO] for x in TWO for h in EIGHT for l in TWO],
    "x_hi": [[dp_index(x, h, l, c) for x in TWO] for h in EIGHT for l in TWO for c in TWO],
    "z": [[dp_index(x, h, l, c) for h in EIGHT for l in TWO] for x in TWO for c in TWO],
    "z_hi": [[dp_index(x, h, l, c) for h in EIGHT] for x in TWO for l in TWO for c in TWO],
    "x_hi z_lo": [[dp_index(x, h, l, c) for x in TWO for l in TWO] for h in EIGHT for c in TWO],
    "core x_hi": [[dp_index(x, h, l, c) for c in TWO for x in TWO] for h in EIGHT for l in TWO],
}


def norm_kernel(x_ref, normed_ref, total_ref):
    values = x_ref[...].astype(jnp.float32)
    centered = values - jnp.mean(values, -1, keepdims=True)
    inv_std = lax.rsqrt(jnp.mean(centered * centered, -1, keepdims=True) + epsilon)
    normed_ref[...] = (centered * inv_std).astype(jnp.bfloat16).reshape(normed_ref.shape)
    total_ref[...] = jnp.sum(values, 1, keepdims=True)


def normalize(layer_input):
    rows, patches, width = layer_input.shape
    return pl.pallas_call(
        norm_kernel,
        grid=(2,),
        in_specs=[pl.BlockSpec((rows // 2, patches, width), lambda i: (i, 0, 0))],
        out_specs=[
            pl.BlockSpec((rows // 2 * patches, width), lambda i: (i, 0)),
            pl.BlockSpec((rows // 2, 1, width), lambda i: (i, 0, 0)),
        ],
        out_shape=[
            jax.ShapeDtypeStruct((rows * patches, width), jnp.bfloat16),
            jax.ShapeDtypeStruct((rows, 1, width), jnp.float32),
        ],
        compiler_params=pltpu.CompilerParams(vmem_limit_bytes=16 * 1024 * 1024),
    )(layer_input)


def hidden_kernel(
    rows, patches, x_ref, in_ref, out_ref, total_ref, slope_ref, act_ref, part_ref, sum_ref
):
    step = pl.program_id(0)
    hidden = jnp.dot(x_ref[...], in_ref[...], preferred_element_type=jnp.float32)
    root = math.sqrt(2.0 / math.pi)
    square = hidden * hidden
    tangent = jnp.tanh(root * (hidden + 0.044715 * square * hidden))
    half = 0.5 * (1.0 + tangent)
    slope_ref[...] = half + 0.5 * hidden * (1.0 - tangent * tangent) * root * (
        1.0 + 3.0 * 0.044715 * square
    )
    width = hidden.shape[1]
    sums = jnp.sum((hidden * half).reshape(-1, rows, patches, width), (0, 2))

    @pl.when(step == 0)
    def _():
        sum_ref[...] = sums

    @pl.when(step > 0)
    def _():
        sum_ref[...] += sums

    @pl.when(step == pl.num_programs(0) - 1)
    def _():
        act_mean = (sum_ref[...] * (1.0 / (8 * patches))).astype(jnp.bfloat16)
        act_ref[...] = act_mean
        part = jnp.dot(act_mean, out_ref[...], preferred_element_type=jnp.float32)
        part = part + total_ref[:, 0] * (1.0 / (8 * patches))
        part_ref[...] = jnp.broadcast_to(part.astype(jnp.bfloat16)[None], part_ref.shape)


def hidden_layer(flat, full_in, out_weight, totals, patches):
    tokens, width = flat.shape
    units = full_in.shape[1]
    rows = totals.shape[0]
    block = 4 * rows * patches
    return pl.pallas_call(
        functools.partial(hidden_kernel, rows, patches),
        grid=(tokens // block,),
        in_specs=[
            pl.BlockSpec((block, width), lambda i: (i, 0)),
            pl.BlockSpec((width, units), lambda i: (0, 0)),
            pl.BlockSpec((units, width), lambda i: (0, 0)),
            pl.BlockSpec((rows, 1, width), lambda i: (0, 0, 0)),
        ],
        out_specs=[
            pl.BlockSpec((block, units), lambda i: (i, 0)),
            pl.BlockSpec((rows, units), lambda i: (0, 0)),
            pl.BlockSpec((8, rows, width), lambda i: (0, 0, 0)),
        ],
        out_shape=[
            jax.ShapeDtypeStruct((tokens, units), jnp.float32),
            jax.ShapeDtypeStruct((rows, units), jnp.bfloat16),
            jax.ShapeDtypeStruct((8, rows, width), jnp.bfloat16),
        ],
        scratch_shapes=[pltpu.VMEM((rows, units), jnp.float32)],
        compiler_params=pltpu.CompilerParams(vmem_limit_bytes=60 * 1024 * 1024),
    )(flat, full_in, out_weight, totals)


def unit_rows(values):
    norm_inv = lax.rsqrt(jnp.sum(values * values, -1, keepdims=True) + epsilon)
    return (values * norm_inv, norm_inv)


def unit_backward(grad_dir, unit_vals, norm_inv):
    return (grad_dir - unit_vals * jnp.sum(unit_vals * grad_dir, -1, keepdims=True)) * norm_inv


def exchange(blocks, axis):
    if axis in GROUPS:
        return lax.all_to_all(blocks, "dp", 0, 0, axis_index_groups=GROUPS[axis], tiled=True)
    return lax.all_to_all(blocks, axis, 0, 0, tiled=True)


def spread(block, axis):
    count = len(GROUPS[axis][0]) if axis in GROUPS else lax.axis_size(axis)
    return exchange(jnp.broadcast_to(block[None], (count,) + block.shape), axis)


def pair(block, axis):
    index = lax.axis_index("dp")
    first = (index % 2 if axis == "core" else index // 32) == 0
    other = lax.ppermute(block, "dp", [p for a, b in GROUPS[axis] for p in ((a, b), (b, a))])
    return jnp.stack([jnp.where(first, block, other), jnp.where(first, other, block)])


def sum_over(block, axis):
    return jnp.sum(spread(block, axis).astype(jnp.float32), 0)


def gather_z(block):
    return lax.all_gather(block, "dp", axis=0, axis_index_groups=GROUPS["z"], tiled=False)


def body(
    layer_input, in_weight, out_weight, image_rest, text_embed, log_scale, logit_bias, loss_scale
):
    local_rows, local_patches, width_model = layer_input.shape
    hidden_width = in_weight.shape[1]
    patches = local_patches * 8
    dp_count = 64
    in_rows = in_weight.shape[0]
    text_count = text_embed.shape[0]
    text_rows = text_count * width_model // hidden_width
    scale_value = jnp.exp(log_scale[0])
    image_count = local_rows + image_rest.shape[0]
    weight_coef = loss_scale[0] / (image_count * dp_count)

    normed, totals = normalize(layer_input)
    token_shape = (8, local_rows, local_patches, hidden_width)

    text_unit, text_inv = unit_rows(text_embed.astype(jnp.float32))
    text_low = text_unit.astype(jnp.bfloat16)
    in_weight, normed = lax.optimization_barrier((in_weight, normed))
    near = pair(in_weight, "x_hi").reshape(2 * in_rows, hidden_width)
    near = jnp.concatenate([near, text_low.reshape(text_rows, hidden_width)], 0)
    flat = lax.all_gather(normed, "mp", axis=0, tiled=True)
    both = gather_z(near)
    full_in = pair(both[:, : 2 * in_rows], "core").reshape(2, 16, 2, in_rows, hidden_width)
    full_in = jnp.transpose(full_in, (2, 1, 0, 3, 4)).reshape(width_model, hidden_width)
    texts = spread(both[:, 2 * in_rows :], "core x_hi")

    first_row = lax.axis_index("mp") * text_count
    zero_index = jnp.zeros((), jnp.int32)
    paired_texts = lax.dynamic_update_slice(
        jnp.zeros((image_count, width_model), jnp.float32),
        text_low.astype(jnp.float32),
        (first_row, zero_index),
    )
    slope, act_mean, part_pool = hidden_layer(flat, full_in, out_weight, totals, local_patches)
    texts = jnp.transpose(texts.reshape(4, 8, 2, text_rows, hidden_width), (0, 2, 1, 3, 4))
    texts = texts.reshape(dp_count * text_count, width_model)
    pooled_parts, texts = lax.optimization_barrier((exchange(part_pool, "mp"), texts))
    pooled = jnp.sum(pooled_parts.astype(jnp.float32), 0)
    images = jnp.concatenate([pooled, image_rest.astype(jnp.float32)], 0)
    image_unit, image_inv = unit_rows(images)
    image_low = image_unit.astype(jnp.bfloat16)
    logits = (
        scale_value * jnp.einsum("id,jd->ij", image_low, texts, preferred_element_type=jnp.float32)
        + logit_bias[0]
    )
    pair_weights = (weight_coef * jax.nn.sigmoid(logits)).astype(jnp.bfloat16)
    image_acc = jnp.dot(pair_weights, texts, preferred_element_type=jnp.float32)
    image_dir = scale_value * sum_over(
        (image_acc - weight_coef * paired_texts).astype(jnp.bfloat16), "mp"
    )
    image_grad = unit_backward(image_dir, image_unit, image_inv)
    pool_grad = image_grad[:local_rows]
    rest_grad = image_grad[local_rows:]
    pool_low = pool_grad.astype(jnp.bfloat16)
    row_grad = (
        jnp.einsum("bd,fd->bf", pool_low, out_weight, preferred_element_type=jnp.float32) / patches
    )
    hidden_grad = (
        (row_grad.reshape(1, local_rows, 1, hidden_width) * slope.reshape(token_shape))
        .astype(jnp.bfloat16)
        .reshape(-1, hidden_width)
    )

    text_part = jnp.einsum("ij,id->jd", pair_weights, image_low, preferred_element_type=jnp.float32)
    in_part = jnp.einsum("rd,rf->df", flat, hidden_grad, preferred_element_type=jnp.float32)
    index = lax.axis_index("dp")
    place = index % 2 * 4 + index // 32 * 2 + index // 2 % 2
    column_width = width_model // dp_count
    columns = pool_low.reshape(local_rows, 2, 8, 2, 2, column_width)
    columns = jnp.transpose(columns, (4, 1, 3, 2, 0, 5)).reshape(2, 4, 8, local_rows, column_width)
    columns = jnp.concatenate([columns] * 8, -1)
    columns = jnp.where(jnp.arange(8 * column_width) // column_width == place, columns, 0)
    columns = jnp.pad(columns, [(0, 0)] * 4 + [(0, hidden_width - columns.shape[-1])])
    parts = jnp.concatenate(
        [
            in_part.astype(jnp.bfloat16).reshape(2, 4, 8, in_rows, hidden_width),
            text_part.astype(jnp.bfloat16).reshape(2, 4, 8, text_rows, hidden_width),
            columns,
        ],
        3,
    )
    for axis in ("core", "x_hi z_lo"):
        got = exchange(parts, axis)
        parts = sum(got[k].astype(jnp.float32) for k in range(got.shape[0])).astype(jnp.bfloat16)
    normed_part = jnp.einsum(
        "rf,df->rd", hidden_grad, full_in, preferred_element_type=jnp.float32
    ).astype(jnp.bfloat16)
    normed_part, parts = lax.optimization_barrier((normed_part, parts))
    normed_grad = (
        lax.psum_scatter(normed_part, "mp", scatter_dimension=0, tiled=True)
        .astype(jnp.float32)
        .reshape(layer_input.shape)
    )
    got = exchange(parts, "z_hi")
    summed = jnp.sum(got[:, : in_rows + text_rows].astype(jnp.float32), 0)
    means = pair(act_mean, "core").reshape(2 * local_rows, hidden_width)
    back = jnp.concatenate([summed[:in_rows].astype(jnp.bfloat16), means], 0)
    normed_grad, again = lax.optimization_barrier((normed_grad, layer_input))
    inputs_f = again.astype(jnp.float32)
    centered = inputs_f - jnp.mean(inputs_f, -1, keepdims=True)
    inv_std = lax.rsqrt(jnp.mean(centered * centered, -1, keepdims=True) + epsilon)
    standard = centered * inv_std
    input_grad = inv_std * (
        normed_grad
        - jnp.mean(normed_grad, -1, keepdims=True)
        - standard * jnp.mean(normed_grad * standard, -1, keepdims=True)
    )
    input_grad = (input_grad + pool_grad[:, None, :] / patches).astype(jnp.bfloat16)
    back = spread(spread(back, "z_hi"), "x_hi z_lo")
    back, input_grad = lax.optimization_barrier((back, input_grad))
    back = back.reshape(dp_count // 2, -1, hidden_width)
    in_weight_grad = pair(back[:, :in_rows], "core").reshape(width_model, hidden_width)
    all_means = back[:, in_rows:].reshape(-1, hidden_width)
    columns = got[:, in_rows + text_rows :, : 8 * column_width]
    columns = columns.reshape(8, local_rows, 2, 4, column_width)
    columns = jnp.transpose(columns, (3, 0, 2, 1, 4)).reshape(-1, column_width)
    out_weight_grad = jnp.einsum(
        "bf,bc->fc", all_means, columns, preferred_element_type=jnp.float32
    ).astype(jnp.bfloat16)

    text_acc = summed[in_rows:].reshape(text_count, width_model)
    paired_images = lax.dynamic_slice_in_dim(image_low, first_row, text_count, 0).astype(
        jnp.float32
    )
    text_dir = scale_value * (text_acc - weight_coef * paired_images)
    text_grad = unit_backward(text_dir, text_unit, text_inv)

    return (input_grad, in_weight_grad, out_weight_grad, rest_grad, text_grad)


def solution(mesh):
    in_specs = (
        P("dp", "mp", None),
        P("dp", "mp"),
        P("mp", None),
        P("dp", None),
        P(("dp", "mp"), None),
        P(),
        P(),
        P(),
    )
    out_specs = (
        P("dp", "mp", None),
        P(None, "mp"),
        P("mp", "dp"),
        P("dp", None),
        P(("dp", "mp"), None),
    )
    return jax.shard_map(body, mesh=mesh, in_specs=in_specs, out_specs=out_specs, check_vma=False)
```
